512 devices in a mesh: bead: 32 (over z, x), space: 16 (over y, core).
Axes of the slice: x: 4, y: 8, z: 8, core: 2. Of those that a mesh axis runs over, the one named last changes fastest.
Arguments:
- positions: float32 [32, 3, 65536], P('bead', None, 'space'), may hold values from -5 to 5
- momenta: float32 [32, 3, 65536], P('bead', None, 'space'), may hold values from -6 to 6
- forces: float32 [32, 3, 65536], P('bead', None, 'space'), may hold values from -6 to 6
- noise: float32 [32, 3, 65536], P('bead', None, 'space'), may hold values from -6 to 6
- species: int32 [65536], P('space'), may hold values from 0 to 3
- block_pairs: int32 [2, 16384], P(None, 'space'), may hold values from 0 to 71, as said below
- pair_count: int32 [16], P('space'), may hold values from 128 to 1024, as said below
- halo_blocks: int32 [2, 64], P(None, 'space'), may hold values from 0 to 63, as said below
Outputs:
- positions_new: float32 [32, 3, 65536], P('bead', None, 'space')
- momenta_new: float32 [32, 3, 65536], P('bead', None, 'space')
- forces_new: float32 [32, 3, 65536], P('bead', None, 'space')
The draws below stay inside these ranges and needn't reach their ends.
Inputs may be any that keep to these rules, and one draw needn't show every extreme that they name: `block_pairs`: columns 1024 * s to 1024 * (s + 1) - 1 belong to shard s; row 0 is a local block number below 64, row 1 an extended block number of that shard. `pair_count`: some shard uses all 1024 slots. `halo_blocks`: columns 4 * s to 4 * (s + 1) - 1 belong to shard s; the 8 numbers of a shard are distinct local block numbers.
All inputs are finite; a program needn't handle non-finite values.
Results may differ from the reference program's by a relative error of at most 0.0003.
Values sent between devices are 32-bit elements; how exact they have to be, the bound alone decides.
A program may use at most 64 MiB of HBM per device.

```python
import jax
import jax.numpy as jnp
from jax import lax

P_SIZE = 32
BLOCK = 64
HB = 4
BLK_DEV = 64
PAIR_DEV = 1024
ATOMS = 65536
N_SPACE = 16


def draw_positions(key, part):
    first_key, second_key, third_key, fourth_key = jax.random.split(key, 4)
    centre = jnp.clip(jax.random.normal(first_key, (3, ATOMS), jnp.float32), -4.0, 4.0)
    phase_common = jax.random.uniform(third_key, (3, 1), jnp.float32, -jnp.pi, jnp.pi)
    jitter = 0.3 * jax.random.uniform(fourth_key, (3, ATOMS), jnp.float32, -1.0, 1.0)
    bead_float = jnp.arange(P_SIZE, dtype=jnp.int32).astype(jnp.float32)[:, None, None]
    wave = 1.5 * jnp.cos(2.0 * jnp.pi * 5.0 * bead_float / P_SIZE + phase_common[None] + jitter[None])
    offsets = wave + 0.25 * jnp.clip(jax.random.normal(second_key, (P_SIZE, 3, ATOMS), jnp.float32), -4.0, 4.0)
    return jnp.clip(centre[None] + offsets, -5.0, 5.0).astype(jnp.float32)


def draw_block_pairs(key, part):
    first_key, second_key = jax.random.split(key)
    local_ids = jax.random.randint(first_key, (1, PAIR_DEV * N_SPACE), 0, BLK_DEV, dtype=jnp.int32)
    partner_ids = jax.random.randint(second_key, (1, PAIR_DEV * N_SPACE), 0, BLK_DEV + 2 * HB, dtype=jnp.int32)
    return jnp.concatenate([local_ids, partner_ids], axis=0)


def draw_pair_count(key, part):
    first_key, second_key = jax.random.split(key)
    counts = jax.random.randint(first_key, (N_SPACE,), PAIR_DEV // 8, PAIR_DEV // 2 + 1, dtype=jnp.int32)
    busiest = jax.random.randint(second_key, (), 0, N_SPACE, dtype=jnp.int32)
    return jnp.where(jnp.arange(N_SPACE, dtype=jnp.int32) == busiest, PAIR_DEV, counts).astype(jnp.int32)


def draw_halo_blocks(key, part):
    shard_keys = jax.random.split(key, N_SPACE)
    chosen = jax.vmap(lambda shard_key: jax.random.permutation(shard_key, BLK_DEV)[:2 * HB])(shard_keys)
    return chosen.reshape(N_SPACE, 2, HB).transpose(1, 0, 2).reshape(2, N_SPACE * HB).astype(jnp.int32)


def set_ends(values, rng, smallest, largest):
    dims = values.shape
    index_at = [jax.random.randint(jax.random.fold_in(rng, axis), (), 0, dims[axis]) for axis in range(len(dims))]
    values = values.at[tuple(index_at)].set(smallest)
    longest = dims.index(max(dims))
    index_at[longest] = (index_at[longest] + 1) % dims[longest]
    return values.at[tuple(index_at)].set(largest)


def levels(key, shape, shards, least, top_value):
    loudness = 1.0
    for axis_at, blocks in shards:
        steps = jax.random.uniform(jax.random.fold_in(jax.random.fold_in(key, 6), axis_at), (blocks,), jnp.float32, least / len(shards), top_value / len(shards))
        loudness = loudness * jnp.repeat(jnp.exp(steps), shape[axis_at] // blocks).reshape((-1,) + (1,) * (len(shape) - 1 - axis_at))
    return loudness


def gaussian(key, shape, deviation, most, cuts=(), held_as=jnp.bfloat16):
    array = deviation * jax.random.normal(key, shape, jnp.float32)
    if cuts:
        array = array * levels(key, shape, cuts, -0.22, 0.18)
    return jnp.clip(array, -most, most).astype(held_as)


def setup_inputs(seed: int = 0) -> dict:
    keys = jax.random.split(jax.random.key(seed), 9)
    return {
        "positions": draw_positions(jax.random.fold_in(keys[8], 71), 0),
        "momenta": gaussian(keys[1], (P_SIZE, 3, ATOMS), 1.0, 6.0, ((0, 32), (2, 16)), jnp.float32),
        "forces": gaussian(keys[2], (P_SIZE, 3, ATOMS), 1.0, 6.0, ((0, 32), (2, 16)), jnp.float32),
        "noise": gaussian(keys[3], (P_SIZE, 3, ATOMS), 1.0, 6.0, ((0, 32), (2, 16)), jnp.float32),
        "species": set_ends(jax.random.randint(keys[4], (ATOMS,), 0, 4), jax.random.fold_in(keys[4], 1), 0, 3).astype(jnp.int32),
        "block_pairs": draw_block_pairs(jax.random.fold_in(keys[8], 71), 0),
        "pair_count": draw_pair_count(jax.random.fold_in(keys[8], 71), 0),
        "halo_blocks": draw_halo_blocks(jax.random.fold_in(keys[8], 71), 0),
    }


eps_pair = 0.01
time_step = 0.5
gamma_centroid = 0.5
pair_group = 16
mass_values = (1.0, 0.3, 2.5, 0.75)
strength_values = (1.0, 0.5, 1.5, 0.8)
reach_values = (1.0, 0.6, 1.4, 0.9)
highest = lax.Precision.HIGHEST

def lookup(values_list, species):
    result = jnp.zeros(species.shape, jnp.float32)
    for species_kind in range(4):
        result = result + jnp.where(species == species_kind, values_list[species_kind], 0.0).astype(jnp.float32)
    return result

def modes_matrix(bead_count):
    steps_int = jnp.arange(bead_count, dtype=jnp.int32)
    product_mod = steps_int[:, None] * steps_int[None, :] % bead_count
    phase_angle = 2.0 * jnp.pi * product_mod.astype(jnp.float32) / bead_count
    mode_grid = jnp.broadcast_to(steps_int[None, :], (bead_count, bead_count))
    bead_grid = jnp.broadcast_to(steps_int[:, None], (bead_count, bead_count))
    half_modes = bead_count // 2
    root_one = jnp.sqrt(jnp.float32(1.0 / bead_count))
    root_two = jnp.sqrt(jnp.float32(2.0 / bead_count))
    matrix = jnp.where(mode_grid < half_modes, root_two * jnp.cos(phase_angle), root_two * jnp.sin(phase_angle))
    matrix = jnp.where(mode_grid == 0, root_one, matrix)
    alternating = jnp.where(bead_grid % 2 == 0, root_one, -root_one)
    matrix = jnp.where(mode_grid == half_modes, alternating, matrix)
    return matrix.astype(jnp.float32)

def propagate(q_modes, p_modes, noise_modes, masses, mode_numbers, bead_count):
    mode_float = mode_numbers.astype(jnp.float32)[:, None, None]
    centroid = (mode_numbers == 0)[:, None, None]
    frequency = 2.0 * jnp.sin(jnp.pi * mode_float / bead_count)
    friction = jnp.where(centroid, gamma_centroid, 2.0 * frequency)
    damping = jnp.exp(-friction * time_step)
    spread = jnp.sqrt(1.0 - damping * damping)
    p_mixed = damping * p_modes + spread * jnp.sqrt(masses) * noise_modes
    safe_freq = jnp.where(centroid, 1.0, frequency)
    cosine = jnp.cos(frequency * time_step)
    sine_term = jnp.sin(frequency * time_step)
    q_cycle = cosine * q_modes + sine_term / (masses * safe_freq) * p_mixed
    p_cycle = -masses * safe_freq * sine_term * q_modes + cosine * p_mixed
    q_next = jnp.where(centroid, q_modes + time_step * p_mixed / masses, q_cycle)
    p_next = jnp.where(centroid, p_mixed, p_cycle)
    return (q_next, p_next)

def group_force(pos_i, pos_j, par_i, par_j, live_mask):
    pair_width = par_i[1][:, :, None] + par_j[1][:, None, :]
    weight_base = eps_pair * 2.0 * par_i[0][:, :, None] * par_j[0][:, None, :] / pair_width * live_mask[:, None, None]
    norm_i = lax.optimization_barrier(jnp.sum(pos_i * pos_i, axis=1))
    norm_j = lax.optimization_barrier(jnp.sum(pos_j * pos_j, axis=1))
    cross_term = jnp.einsum('bcgi,bcgj->bgij', pos_i, pos_j, precision=highest)
    distance = norm_i[..., :, None] + norm_j[..., None, :] - 2.0 * cross_term
    weight = weight_base[None] * jnp.exp(-distance / pair_width[None])
    weight_sum = lax.optimization_barrier(jnp.sum(weight, axis=3))
    pulled = jnp.einsum('bgij,bcgj->bcgi', weight, pos_j, precision=highest)
    return pos_i * weight_sum[:, None] - pulled

def pair_forces(new_positions, strength, reach, block_pairs, pair_count, halo_blocks):
    bead_count = new_positions.shape[0]
    position_blocks = new_positions.reshape(bead_count, 3, N_SPACE, BLK_DEV, BLOCK)
    param_blocks = jnp.stack([strength, reach]).reshape(2, N_SPACE, BLK_DEV, BLOCK)
    sent_lists = halo_blocks.reshape(2, N_SPACE, HB)
    pair_lists = block_pairs.reshape(2, N_SPACE, PAIR_DEV)

    def one_shard(shard_index):
        lower = jnp.maximum(shard_index - 1, 0).astype(jnp.int32)
        upper = jnp.minimum(shard_index + 1, N_SPACE - 1).astype(jnp.int32)
        lower_ok = (shard_index > 0).astype(jnp.float32)
        upper_ok = (shard_index < N_SPACE - 1).astype(jnp.float32)
        lower_ids = lax.dynamic_index_in_dim(sent_lists[1], lower, 0, False)
        upper_ids = lax.dynamic_index_in_dim(sent_lists[0], upper, 0, False)
        own_pos = lax.dynamic_index_in_dim(position_blocks, shard_index, 2, False)
        own_par = lax.dynamic_index_in_dim(param_blocks, shard_index, 1, False)
        lower_pos = jnp.take(lax.dynamic_index_in_dim(position_blocks, lower, 2, False), lower_ids, axis=2) * lower_ok
        upper_pos = jnp.take(lax.dynamic_index_in_dim(position_blocks, upper, 2, False), upper_ids, axis=2) * upper_ok
        lower_par = jnp.take(lax.dynamic_index_in_dim(param_blocks, lower, 1, False), lower_ids, axis=1) * lower_ok
        upper_par = jnp.take(lax.dynamic_index_in_dim(param_blocks, upper, 1, False), upper_ids, axis=1) * upper_ok
        ext_pos = jnp.concatenate([lower_pos, own_pos, upper_pos], axis=2)
        ext_par = jnp.concatenate([lower_par, own_par, upper_par], axis=1)
        shard_pairs = lax.dynamic_index_in_dim(pair_lists, shard_index, 1, False)
        live_count = lax.dynamic_index_in_dim(pair_count, shard_index, 0, False)

        def add_group(group, totals):
            pair_ids = lax.dynamic_slice_in_dim(shard_pairs, (group * pair_group).astype(jnp.int32), pair_group, 1)
            slots = group * pair_group + jnp.arange(pair_group, dtype=jnp.int32)
            live_mask = (slots < live_count).astype(jnp.float32)
            first_ids = pair_ids[0] + HB
            pos_i = jnp.take(ext_pos, first_ids, axis=2)
            pos_j = jnp.take(ext_pos, pair_ids[1], axis=2)
            par_i = jnp.take(ext_par, first_ids, axis=1)
            par_j = jnp.take(ext_par, pair_ids[1], axis=1)
            force_part = group_force(pos_i, pos_j, par_i, par_j, live_mask)
            one_hot = (pair_ids[0][:, None] == jnp.arange(BLK_DEV, dtype=jnp.int32)[None, :]).astype(jnp.float32)
            return totals + jnp.einsum('bcgi,gk->bcki', force_part, one_hot, precision=highest)
        zero_start = jnp.zeros((bead_count, 3, BLK_DEV, BLOCK), jnp.float32)
        return lax.fori_loop(0, PAIR_DEV // pair_group, add_group, zero_start)
    per_shard = lax.map(one_shard, jnp.arange(N_SPACE, dtype=jnp.int32))
    return per_shard.transpose(1, 2, 0, 3, 4).reshape(bead_count, 3, N_SPACE * BLK_DEV * BLOCK)

def reference(positions, momenta, forces, noise, species, block_pairs, pair_count, halo_blocks):
    bead_count = positions.shape[0]
    masses = lookup(mass_values, species)
    strength = lookup(strength_values, species)
    reach = lookup(reach_values, species)
    matrix = modes_matrix(bead_count)
    p_half = momenta + 0.5 * time_step * forces
    q_modes = jnp.einsum('jk,jcn->kcn', matrix, positions, precision=highest)
    p_modes = jnp.einsum('jk,jcn->kcn', matrix, p_half, precision=highest)
    q_next, p_next = propagate(q_modes, p_modes, noise, masses, jnp.arange(bead_count, dtype=jnp.int32), bead_count)
    positions_new = jnp.einsum('jk,kcn->jcn', matrix, q_next, precision=highest)
    p_mid = jnp.einsum('jk,kcn->jcn', matrix, p_next, precision=highest)
    forces_new = pair_forces(positions_new, strength, reach, block_pairs, pair_count, halo_blocks)
    momenta_new = p_mid + 0.5 * time_step * forces_new
    return (positions_new, momenta_new, forces_new)
```

```python
import functools
import math

import jax
import jax.numpy as jnp
import numpy as np
from jax import lax
from jax.experimental import pallas as pl
from jax.experimental.pallas import tpu as pltpu
from jax.sharding import PartitionSpec as P

BLOCK = 64
LANES = 128
HALO = 4
UNROLL = 4
STEP = 0.5
GAMMA = 0.5
mass_values = (1.0, 0.3, 2.5, 0.75)
strength_values = (1.0, 0.5, 1.5, 0.8)
reach_values = (1.0, 0.6, 1.4, 0.9)
MESH = pl.DeviceIdType.MESH
highest = lax.Precision.HIGHEST


def lookup(values, species):
    out = jnp.full(species.shape, values[3], jnp.float32)
    for k in range(3):
        out = jnp.where(species == k, values[k], out)
    return out


def modes_matrix(n):
    j = np.arange(n)[:, None]
    k = np.arange(n)[None, :]
    phase = 2 * np.pi * (j * k % n) / n
    m = np.where(k < n // 2, np.cos(phase), np.sin(phase)) * math.sqrt(2.0 / n)
    m = np.where(k == 0, math.sqrt(1.0 / n), m)
    m = np.where(k == n // 2, np.where(j % 2 == 0, 1, -1) * math.sqrt(1.0 / n), m)
    return m.astype(np.float32)


def mode_factors(n):
    k = np.arange(n)
    omega = 2 * np.sin(np.pi * k / n)
    gamma = np.where(k == 0, GAMMA, 2 * omega)
    c1 = np.exp(-gamma * STEP)
    c2 = np.sqrt(1 - c1 * c1)
    safe = np.where(k == 0, 1.0, omega)
    drift = np.where(k == 0, STEP, np.sin(omega * STEP) / safe)
    pull = omega * np.sin(omega * STEP)
    turn = np.cos(omega * STEP)
    out = np.zeros((n, LANES), np.float32)
    for c, v in enumerate((c1, c2, turn, drift, pull)):
        out[:, c] = v
    return out


def exchange_kernel(pos_ref, mom_ref, frc_ref, noise_ref, sp_ref, halo_ref, cos_ref, cost_ref, fac_ref,
                    pm_ref, lo_ref, up_ref, slo_ref, sup_ref, hlo_ref, hup_ref,
                    out_buf, in_buf, back_buf, send1, recv1, send2, recv2, nsend, nrecv):
    beads = in_buf.shape[0]
    me = lax.axis_index("bead")
    shard = lax.axis_index("space")
    shards = lax.axis_size("space")
    has_lower = shard > 0
    has_upper = shard < shards - 1

    barrier = pltpu.get_barrier_semaphore()

    def greet(d, _):
        pl.semaphore_signal(barrier, inc=1, device_id={"bead": lax.rem(me + d, beads)}, device_id_type=MESH)
        return 0

    lax.fori_loop(1, beads, greet, 0)

    @pl.when(has_lower)
    def _():
        pl.semaphore_signal(barrier, inc=1, device_id={"space": shard - 1}, device_id_type=MESH)

    @pl.when(has_upper)
    def _():
        pl.semaphore_signal(barrier, inc=1, device_id={"space": shard + 1}, device_id_type=MESH)

    for j in range(beads):
        s = slice(LANES * j, LANES * (j + 1))
        out_buf[j, 0:3] = pos_ref[0, :, s]
        out_buf[j, 3:6] = mom_ref[0, :, s] + (0.5 * STEP) * frc_ref[0, :, s]
        out_buf[j, 6:9] = noise_ref[0, :, s]

    pl.semaphore_wait(barrier, beads - 1 + has_lower.astype(jnp.int32) + has_upper.astype(jnp.int32))

    def first(d):
        j = lax.rem(me + d, beads)
        return pltpu.make_async_remote_copy(
            src_ref=out_buf.at[j, 0:9], dst_ref=in_buf.at[me, 0:9], send_sem=send1.at[j], recv_sem=recv1.at[me],
            device_id={"bead": j}, device_id_type=MESH)

    def second(d):
        j = lax.rem(me + d, beads)
        return pltpu.make_async_remote_copy(
            src_ref=back_buf.at[j, 0:6], dst_ref=pm_ref.at[me, 0:6], send_sem=send2.at[j], recv_sem=recv2.at[me],
            device_id={"bead": j}, device_id_type=MESH)

    def arrived(buf, rows, sem, d):
        j = lax.rem(me + d, beads)
        pltpu.make_async_copy(buf.at[j, 0:rows], buf.at[j, 0:rows], sem.at[j]).wait()

    def each(body):
        def run(d, _):
            body(d)
            return 0
        lax.fori_loop(1, beads, run, 0)

    each(lambda d: first(d).start())
    in_buf[me] = out_buf[me]

    def towards(up):
        to = shard + 1 if up else shard - 1
        k = 3 * int(up)
        ids = {"space": to}

        def copy(src, dst, n):
            return pltpu.make_async_remote_copy(
                src_ref=src, dst_ref=dst, send_sem=nsend.at[k + n], recv_sem=nrecv.at[k + n], device_id=ids,
                device_id_type=MESH)

        def kinds():
            return copy(sp_ref, slo_ref if up else sup_ref, 0)

        def lists():
            return copy(halo_ref, hlo_ref if up else hup_ref, 1)

        def places():
            return copy(pm_ref.at[:, 0:3], lo_ref.at[:, 0:3] if up else up_ref.at[:, 0:3], 2)

        return kinds, lists, places

    for up, there in ((True, has_upper), (False, has_lower)):
        @pl.when(there)
        def _(up=up):
            for c in towards(up)[0:2]:
                c().start()

    each(lambda d: arrived(in_buf, 9, recv1, d))

    def rows(r):
        return in_buf[:, r, :]

    x = jnp.concatenate([rows(r) for r in range(6)], axis=1)
    xi = jnp.concatenate([rows(r) for r in range(6, 9)], axis=1)
    modes = jnp.dot(cost_ref[...], x, precision=highest, preferred_element_type=jnp.float32)
    q, p = modes[:, 0:3 * LANES], modes[:, 3 * LANES:]
    mass = lookup(mass_values, sp_ref[pl.ds(me, 1), :])
    mass3 = jnp.concatenate([mass] * 3, axis=1)
    c1, c2, turn, drift, pull = (fac_ref[:, c:c + 1] for c in range(5))
    mixed = c1 * p + c2 * (jnp.sqrt(mass3) * xi)
    q_next = turn * q + drift * (mixed / mass3)
    p_next = turn * mixed - pull * (mass3 * q)
    beads_out = jnp.dot(cos_ref[...], jnp.concatenate([q_next, p_next], axis=1), precision=highest,
                        preferred_element_type=jnp.float32)
    for r in range(6):
        back_buf[:, r, :] = beads_out[:, LANES * r:LANES * (r + 1)]

    each(lambda d: second(d).start())
    pm_ref[me, 0:6] = back_buf[me, 0:6]
    each(lambda d: arrived(pm_ref, 6, recv2, d))

    for up, there in ((True, has_upper), (False, has_lower)):
        @pl.when(there)
        def _(up=up):
            towards(up)[2]().start()

    each(lambda d: first(d).wait_send())
    each(lambda d: second(d).wait_send())

    for up, there in ((True, has_upper), (False, has_lower)):
        @pl.when(there)
        def _(up=up):
            for c in towards(up):
                c().wait_send()

    for up, there in ((True, has_lower), (False, has_upper)):
        @pl.when(there)
        def _(up=up):
            for c in towards(up):
                c().wait_recv()


def exchange(pos, mom, frc, noise, species, halo):
    beads = lax.axis_size("bead")
    chunks = species.shape[0]
    vmem = pl.BlockSpec(memory_space=pltpu.VMEM)
    f32, i32 = jnp.float32, jnp.int32
    block = jax.ShapeDtypeStruct((chunks, 8, LANES), f32)
    kind = jax.ShapeDtypeStruct(species.shape, i32)
    ids = jax.ShapeDtypeStruct(halo.shape, i32)
    dma = pltpu.SemaphoreType.DMA
    matrix = modes_matrix(beads)
    return pl.pallas_call(
        exchange_kernel,
        out_shape=(block, block, block, kind, kind, ids, ids),
        in_specs=[vmem] * 9,
        out_specs=(vmem,) * 7,
        scratch_shapes=[
            pltpu.VMEM((beads, 16, LANES), f32),
            pltpu.VMEM((beads, 16, LANES), f32),
            pltpu.VMEM((beads, 8, LANES), f32),
            dma((beads,)), dma((beads,)), dma((beads,)), dma((beads,)), dma((6,)), dma((6,)),
        ],
        compiler_params=pltpu.CompilerParams(collective_id=0, has_side_effects=True),
        name="exchange",
    )(pos, mom, frc, noise, species, halo, jnp.asarray(matrix), jnp.asarray(matrix.T), jnp.asarray(mode_factors(beads)))


def force_kernel(pairs_ref, count_ref, hlo_ref, hup_ref, pm_ref, lo_ref, up_ref, sp_ref, slo_ref, sup_ref,
                 pos_ref, mom_ref, frc_ref, tab_j, tab_i, acc, tmp):
    chunks = pm_ref.shape[0]
    blocks = 2 * chunks
    lane = lax.broadcasted_iota(jnp.int32, (32, 128), 1)
    left = lane < 64
    left1 = left[0:8]

    def spread(cols, e):
        for c in range(5):
            b = jnp.broadcast_to(cols[:, c:c + 1], (64, 128))
            tab_j[e, c] = jnp.where(left, b[0:32], b[32:64])

    def packed(rows, species, t):
        xyz = rows[0:3]
        r = lookup(reach_values, species)
        a = lookup(strength_values, species)
        return jnp.concatenate([xyz, r, a, jnp.zeros((3, 128), jnp.float32)], axis=0)

    def own(t, _):
        rows = pm_ref[t]
        m8 = packed(rows, sp_ref[pl.ds(t, 1), :], t)
        cols = m8.T
        spread(cols[0:64], HALO + 2 * t)
        spread(cols[64:128], HALO + 2 * t + 1)
        turned = pltpu.roll(m8, 64, 1)
        for h in range(2):
            both = jnp.where(left1, m8, turned) if h == 0 else jnp.where(left1, turned, m8)
            for c in range(4):
                tab_i[2 * t + h, c] = jnp.broadcast_to(both[c:c + 1], (8, 128))
        for h in range(2):
            for c in range(3):
                acc[2 * t + h, c] = jnp.zeros((8, 128), jnp.float32)
        return 0
    lax.fori_loop(0, chunks, own, 0)

    for side in range(2):
        ids = hlo_ref if side == 0 else hup_ref
        x_ref = lo_ref if side == 0 else up_ref
        s_ref = slo_ref if side == 0 else sup_ref
        there = lax.axis_index("space") > 0 if side == 0 else lax.axis_index("space") < lax.axis_size("space") - 1
        for h in range(HALO):
            b = jnp.where(there, ids[1 - side, h], 0)
            t = b // 2
            m8 = packed(x_ref[t], s_ref[pl.ds(t, 1), :], t)
            m8 = jnp.where(there, m8, 0.0)
            tmp[...] = m8.T
            cols = tmp[pl.ds(pl.multiple_of((b % 2) * 64, 64), 64), :]
            spread(cols, h if side == 0 else HALO + blocks + h)
    tab_j[2 * HALO + blocks] = jnp.zeros(tab_j.shape[1:], jnp.float32)

    live = count_ref[0]

    def pair(p):
        i = pairs_ref[0, p]
        j = jnp.where(p < live, pairs_ref[1, p], 2 * HALO + blocks)
        xi, yi, zi, ri = (tab_i[i, c] for c in range(4))
        f = [None] * 3
        for g in range(4):
            s = pl.ds(8 * g, 8)
            dx = xi - tab_j[j, 0, s]
            dy = yi - tab_j[j, 1, s]
            dz = zi - tab_j[j, 2, s]
            d = dx * dx + dy * dy + dz * dz
            inv = 1.0 / (ri + tab_j[j, 3, s])
            w = jnp.exp(-d * inv) * (inv * tab_j[j, 4, s])
            for k, v in enumerate((dx, dy, dz)):
                f[k] = w * v if g == 0 else f[k] + w * v
        for k in range(3):
            acc[i, k] = acc[i, k] + f[k]

    def group(g, _):
        for u in range(UNROLL):
            pair(g * UNROLL + u)
        return 0
    lax.fori_loop(0, (live + UNROLL - 1) // UNROLL, group, 0)

    def finish(t, _):
        rows = pm_ref[t]
        scale = 0.02 * lookup(strength_values, sp_ref[pl.ds(t, 1), :])
        out = []
        for k in range(3):
            v = [jnp.sum(acc[2 * t + h, k], axis=0, keepdims=True) for h in range(2)]
            v = [x + pltpu.roll(x, 64, 1) for x in v]
            out.append(jnp.where(left[0:1], v[0], v[1]) * scale)
        f = jnp.concatenate(out, axis=0)
        s = pl.ds(pl.multiple_of(t * 128, 128), 128)
        pos_ref[0, :, s] = rows[0:3]
        frc_ref[0, :, s] = f
        mom_ref[0, :, s] = rows[3:6] + 0.25 * f
        return 0
    lax.fori_loop(0, chunks, finish, 0)


def force_call(pairs, count, hlo, hup, pm, lo, up, sp, slo, sup):
    chunks = pm.shape[0]
    smem = pl.BlockSpec(memory_space=pltpu.SMEM)
    vmem = pl.BlockSpec(memory_space=pltpu.VMEM)
    o = jax.ShapeDtypeStruct((1, 3, chunks * 128), jnp.float32)
    return pl.pallas_call(
        force_kernel,
        out_shape=(o, o, o),
        in_specs=[smem] * 4 + [vmem] * 6,
        out_specs=(vmem,) * 3,
        scratch_shapes=[
            pltpu.VMEM((2 * chunks + 2 * HALO + 1, 5, 32, 128), jnp.float32),
            pltpu.VMEM((2 * chunks, 4, 8, 128), jnp.float32),
            pltpu.VMEM((2 * chunks, 3, 8, 128), jnp.float32),
            pltpu.VMEM((128, 8), jnp.float32),
        ],
        compiler_params=pltpu.CompilerParams(vmem_limit_bytes=40 * 2**20),
        name="pair_forces",
    )(pairs, count, hlo, hup, pm, lo, up, sp, slo, sup)


def shards(positions, momenta, forces, noise, species, block_pairs, pair_count, halo_blocks):
    kinds = species.reshape(-1, LANES)
    pm, lo, up, slo, sup, hlo, hup = exchange(positions, momenta, forces, noise, kinds, halo_blocks)
    return force_call(block_pairs, pair_count, hlo, hup, pm, lo, up, kinds, slo, sup)


def solution(mesh):
    big = P("bead", None, "space")
    in_specs = (big, big, big, big, P("space"), P(None, "space"), P("space"), P(None, "space"))
    return jax.shard_map(shards, mesh=mesh, in_specs=in_specs, out_specs=(big, big, big), check_vma=False)
```

```python
import functools
import math

import jax
import jax.numpy as jnp
import numpy as np
from jax import lax
from jax.experimental import pallas as pl
from jax.experimental.pallas import tpu as pltpu
from jax.sharding import PartitionSpec as P

BLOCK = 64
LANES = 128
HALO = 4
UNROLL = 4
STEP = 0.5
GAMMA = 0.5
mass_values = (1.0, 0.3, 2.5, 0.75)
strength_values = (1.0, 0.5, 1.5, 0.8)
reach_values = (1.0, 0.6, 1.4, 0.9)
MESH = pl.DeviceIdType.MESH
highest = lax.Precision.HIGHEST


def lookup(values, species):
    out = jnp.full(species.shape, values[3], jnp.float32)
    for k in range(3):
        out = jnp.where(species == k, values[k], out)
    return out


def modes_matrix(n):
    j = np.arange(n)[:, None]
    k = np.arange(n)[None, :]
    phase = 2 * np.pi * (j * k % n) / n
    m = np.where(k < n // 2, np.cos(phase), np.sin(phase)) * math.sqrt(2.0 / n)
    m = np.where(k == 0, math.sqrt(1.0 / n), m)
    m = np.where(k == n // 2, np.where(j % 2 == 0, 1, -1) * math.sqrt(1.0 / n), m)
    return m.astype(np.float32)


def mode_factors(n):
    k = np.arange(n)
    omega = 2 * np.sin(np.pi * k / n)
    gamma = np.where(k == 0, GAMMA, 2 * omega)
    c1 = np.exp(-gamma * STEP)
    c2 = np.sqrt(1 - c1 * c1)
    safe = np.where(k == 0, 1.0, omega)
    drift = np.where(k == 0, STEP, np.sin(omega * STEP) / safe)
    pull = omega * np.sin(omega * STEP)
    turn = np.cos(omega * STEP)
    out = np.zeros((n, LANES), np.float32)
    for c, v in enumerate((c1, c2, turn, drift, pull)):
        out[:, c] = v
    return out


def exchange_kernel(pos_hbm, mom_hbm, frc_hbm, noise_hbm, sp_ref, halo_ref, cos_ref, cost_ref, fac_ref,
                    pm_hbm, lo_hbm, up_hbm, hlo_ref, hup_ref,
                    raw, out_buf, in_buf, back_buf, pm_ref, load, store, send1, recv1, send2, recv2, nsend, nrecv):
    beads = in_buf.shape[0]
    me = lax.axis_index("bead")
    shard = lax.axis_index("space")
    shards = lax.axis_size("space")
    has_lower = shard > 0
    has_upper = shard < shards - 1

    loads = [pltpu.make_async_copy(src, raw.at[n], load.at[n])
             for n, src in enumerate((pos_hbm, mom_hbm, frc_hbm, noise_hbm))]
    for c in loads:
        c.start()

    barrier = pltpu.get_barrier_semaphore()

    def each(body, unroll=4):
        def run(d, _):
            body(d)
            return 0
        lax.fori_loop(1, beads, run, 0, unroll=unroll)

    each(lambda d: pl.semaphore_signal(
        barrier, inc=1, device_id={"bead": lax.rem(me + d, beads)}, device_id_type=MESH))

    @pl.when(has_lower)
    def _():
        pl.semaphore_signal(barrier, inc=1, device_id={"space": shard - 1}, device_id_type=MESH)

    @pl.when(has_upper)
    def _():
        pl.semaphore_signal(barrier, inc=1, device_id={"space": shard + 1}, device_id_type=MESH)

    for c in loads:
        c.wait()
    for c in range(3):
        s = slice(beads * c, beads * (c + 1))
        out_buf[:, c, :] = raw[0, s]
        out_buf[:, 3 + c, :] = raw[1, s] + (0.5 * STEP) * raw[2, s]
        out_buf[:, 6 + c, :] = raw[3, s]
    kinds = sp_ref[...]
    pm_ref[:, 6, :] = lookup(reach_values, kinds)
    pm_ref[:, 7, :] = lookup(strength_values, kinds)

    pl.semaphore_wait(barrier, beads - 1 + has_lower.astype(jnp.int32) + has_upper.astype(jnp.int32))

    def first(d):
        j = lax.rem(me + d, beads)
        return pltpu.make_async_remote_copy(
            src_ref=out_buf.at[j, 0:9], dst_ref=in_buf.at[me, 0:9], send_sem=send1.at[j], recv_sem=recv1.at[me],
            device_id={"bead": j}, device_id_type=MESH)

    def second(d):
        j = lax.rem(me + d, beads)
        return pltpu.make_async_remote_copy(
            src_ref=back_buf.at[j, 0:6], dst_ref=pm_ref.at[me, 0:6], send_sem=send2.at[j], recv_sem=recv2.at[me],
            device_id={"bead": j}, device_id_type=MESH)

    def arrived(buf, rows, sem, d):
        j = lax.rem(me + d, beads)
        pltpu.make_async_copy(buf.at[j, 0:rows], buf.at[j, 0:rows], sem.at[j]).wait()

    def towards(up, n):
        src, dst = ((halo_ref, hlo_ref if up else hup_ref),
                    (pm_ref.at[:, 3:8], (lo_hbm if up else up_hbm).at[:, 3:8]))[n]
        k = 2 * int(up) + n
        return pltpu.make_async_remote_copy(
            src_ref=src, dst_ref=dst, send_sem=nsend.at[k], recv_sem=nrecv.at[k],
            device_id={"space": shard + 1 if up else shard - 1}, device_id_type=MESH)

    def beside(n, act, receiving=False):
        for up, there in ((True, has_upper), (False, has_lower)):
            if receiving:
                there = has_lower if up else has_upper

            @pl.when(there)
            def _(up=up):
                act(towards(up, n))

    each(lambda d: first(d).start())
    beside(0, lambda c: c.start())
    in_buf[me] = out_buf[me]
    each(lambda d: arrived(in_buf, 9, recv1, d))

    x = jnp.concatenate([in_buf[:, r, :] for r in range(6)], axis=1)
    xi = jnp.concatenate([in_buf[:, r, :] for r in range(6, 9)], axis=1)
    modes = jnp.dot(cost_ref[...], x, precision=highest, preferred_element_type=jnp.float32)
    q, p = modes[:, 0:3 * LANES], modes[:, 3 * LANES:]
    mass = lookup(mass_values, sp_ref[pl.ds(me, 1), :])
    mass3 = jnp.concatenate([mass] * 3, axis=1)
    c1, c2, turn, drift, pull = (fac_ref[:, c:c + 1] for c in range(5))
    mixed = c1 * p + c2 * (jnp.sqrt(mass3) * xi)
    q_next = turn * q + drift * (mixed / mass3)
    p_next = turn * mixed - pull * (mass3 * q)
    beads_out = jnp.dot(cos_ref[...], jnp.concatenate([p_next, q_next], axis=1), precision=highest,
                        preferred_element_type=jnp.float32)
    for r in range(6):
        back_buf[:, r, :] = beads_out[:, LANES * r:LANES * (r + 1)]

    each(lambda d: second(d).start())
    pm_ref[me, 0:6] = back_buf[me, 0:6]
    each(lambda d: arrived(pm_ref, 6, recv2, d))

    keep = pltpu.make_async_copy(pm_ref, pm_hbm, store.at[0])
    keep.start()
    beside(1, lambda c: c.start())
    each(lambda d: first(d).wait_send())
    beside(0, lambda c: c.wait_send())
    beside(0, lambda c: c.wait_recv(), True)
    each(lambda d: second(d).wait_send())
    beside(1, lambda c: c.wait_send())
    beside(1, lambda c: c.wait_recv(), True)
    keep.wait()


def exchange(pos, mom, frc, noise, species, halo):
    beads = lax.axis_size("bead")
    chunks = species.shape[0]
    vmem = pl.BlockSpec(memory_space=pltpu.VMEM)
    hbm = pl.BlockSpec(memory_space=pl.ANY)
    f32 = jnp.float32
    block = jax.ShapeDtypeStruct((chunks, 8, LANES), f32)
    ids = jax.ShapeDtypeStruct(halo.shape, jnp.int32)
    dma = pltpu.SemaphoreType.DMA
    matrix = modes_matrix(beads)
    return pl.pallas_call(
        exchange_kernel,
        out_shape=(block, block, block, ids, ids),
        in_specs=[hbm] * 4 + [vmem] * 5,
        out_specs=(hbm,) * 3 + (vmem,) * 2,
        scratch_shapes=[
            pltpu.VMEM((4, 3 * chunks, LANES), f32),
            pltpu.VMEM((beads, 16, LANES), f32),
            pltpu.VMEM((beads, 16, LANES), f32),
            pltpu.VMEM((beads, 8, LANES), f32),
            pltpu.VMEM((chunks, 8, LANES), f32),
            dma((4,)), dma((1,)), dma((beads,)), dma((beads,)), dma((beads,)), dma((beads,)), dma((4,)), dma((4,)),
        ],
        compiler_params=pltpu.CompilerParams(collective_id=0, has_side_effects=True),
        name="exchange",
    )(pos, mom, frc, noise, species, halo, jnp.asarray(matrix), jnp.asarray(matrix.T), jnp.asarray(mode_factors(beads)))


def force_kernel(pairs_ref, count_ref, hlo_ref, hup_ref, pm_hbm, lo_hbm, up_hbm, pos_ref, mom_ref, frc_ref,
                 tab_j, tab_i, acc, pm_ref, halo, tmp, sem):
    chunks = pm_ref.shape[0]
    blocks = 2 * chunks
    left = lax.broadcasted_iota(jnp.int32, (32, LANES), 1) < 64
    left1 = left[0:8]
    get_own = pltpu.make_async_copy(pm_hbm, pm_ref, sem.at[0])
    get_own.start()
    sides = []
    shard = lax.axis_index("space")
    for side in range(2):
        there = shard > 0 if side == 0 else shard < lax.axis_size("space") - 1
        for h in range(HALO):
            b = jnp.where(there, (hup_ref if side else hlo_ref)[1 - side, h], 0)
            get = pltpu.make_async_copy((up_hbm if side else lo_hbm).at[b // 2], halo.at[side * HALO + h], sem.at[1 + side * HALO + h])
            get.start()
            sides.append((get, there, b % 2))

    def clear(i, _):
        for c in range(3):
            acc[i, c] = jnp.zeros((8, LANES), jnp.float32)
        return 0
    lax.fori_loop(0, blocks, clear, 0, unroll=8)
    tab_j[2 * HALO + blocks] = jnp.zeros(tab_j.shape[1:], jnp.float32)

    def spread(cols, e):
        for c in range(5):
            b = jnp.broadcast_to(cols[:, 3 + c:4 + c], (64, LANES))
            tab_j[e, c] = jnp.where(left, b[0:32], b[32:64])

    get_own.wait()

    def own(t, _):
        m8 = pm_ref[t]
        cols = m8.T
        spread(cols[0:64], HALO + 2 * t)
        spread(cols[64:128], HALO + 2 * t + 1)
        turned = pltpu.roll(m8, 64, 1)
        for h in range(2):
            both = jnp.where(left1, m8, turned) if h == 0 else jnp.where(left1, turned, m8)
            for c in range(4):
                tab_i[2 * t + h, c] = jnp.broadcast_to(both[3 + c:4 + c], (8, LANES))
        return 0
    lax.fori_loop(0, chunks, own, 0, unroll=8)

    for n, (get, there, half) in enumerate(sides):
        get.wait()
        tmp[n] = jnp.where(there, halo[n], 0.0).T
        cols = tmp[n, pl.ds(pl.multiple_of(half * 64, 64), 64), :]
        spread(cols, n if n < HALO else blocks + n)

    live = count_ref[0]

    def pair(p):
        i = pairs_ref[0, p]
        j = jnp.where(p < live, pairs_ref[1, p], 2 * HALO + blocks)
        xi, yi, zi, ri = (tab_i[i, c] for c in range(4))
        f = [None] * 3
        for g in range(4):
            s = pl.ds(8 * g, 8)
            dx = xi - tab_j[j, 0, s]
            dy = yi - tab_j[j, 1, s]
            dz = zi - tab_j[j, 2, s]
            d = dx * dx + dy * dy + dz * dz
            inv = 1.0 / (ri + tab_j[j, 3, s])
            w = jnp.exp(-d * inv) * (inv * tab_j[j, 4, s])
            for k, v in enumerate((dx, dy, dz)):
                f[k] = w * v if g == 0 else f[k] + w * v
        for k in range(3):
            acc[i, k] = acc[i, k] + f[k]

    def group(g, _):
        for u in range(UNROLL):
            pair(g * UNROLL + u)
        return 0
    lax.fori_loop(0, (live + UNROLL - 1) // UNROLL, group, 0)

    def finish(t, _):
        rows = pm_ref[t]
        scale = 0.02 * rows[7:8]
        for k in range(3):
            v = [jnp.sum(acc[2 * t + h, k], axis=0, keepdims=True) for h in range(2)]
            v = [x + pltpu.roll(x, 64, 1) for x in v]
            f = jnp.where(left[0:1], v[0], v[1]) * scale
            at = pl.ds(k * chunks + t, 1)
            pos_ref[at, :] = rows[3 + k:4 + k]
            frc_ref[at, :] = f
            mom_ref[at, :] = rows[k:k + 1] + 0.25 * f
        return 0
    lax.fori_loop(0, chunks, finish, 0, unroll=8)


def force_call(pairs, count, hlo, hup, pm, lo, up):
    chunks = pm.shape[0]
    smem = pl.BlockSpec(memory_space=pltpu.SMEM)
    vmem = pl.BlockSpec(memory_space=pltpu.VMEM)
    hbm = pl.BlockSpec(memory_space=pl.ANY)
    o = jax.ShapeDtypeStruct((3 * chunks, LANES), jnp.float32)
    return pl.pallas_call(
        force_kernel,
        out_shape=(o, o, o),
        in_specs=[smem] * 4 + [hbm] * 3,
        out_specs=(vmem,) * 3,
        scratch_shapes=[
            pltpu.VMEM((2 * chunks + 2 * HALO + 1, 5, 32, LANES), jnp.float32),
            pltpu.VMEM((2 * chunks, 4, 8, LANES), jnp.float32),
            pltpu.VMEM((2 * chunks, 3, 8, LANES), jnp.float32),
            pltpu.VMEM((chunks, 8, LANES), jnp.float32),
            pltpu.VMEM((2 * HALO, 8, LANES), jnp.float32),
            pltpu.VMEM((2 * HALO, LANES, 8), jnp.float32),
            pltpu.SemaphoreType.DMA((1 + 2 * HALO,)),
        ],
        compiler_params=pltpu.CompilerParams(vmem_limit_bytes=60 * 2**20),
        name="pair_forces",
    )(pairs, count, hlo, hup, pm, lo, up)


def shards(positions, momenta, forces, noise, species, block_pairs, pair_count, halo_blocks):
    flat = [a.reshape(-1, LANES) for a in (positions, momenta, forces, noise)]
    pm, lo, up, hlo, hup = exchange(*flat, species.reshape(-1, LANES), halo_blocks)
    outs = force_call(block_pairs, pair_count, hlo, hup, pm, lo, up)
    return tuple(o.reshape(positions.shape) for o in outs)


def solution(mesh):
    big = P("bead", None, "space")
    in_specs = (big, big, big, big, P("space"), P(None, "space"), P("space"), P(None, "space"))
    return jax.shard_map(shards, mesh=mesh, in_specs=in_specs, out_specs=(big, big, big), check_vma=False)
```

```python
import functools
import math

import jax
import jax.numpy as jnp
import numpy as np
from jax import lax
from jax.experimental import pallas as pl
from jax.experimental.pallas import tpu as pltpu
from jax.sharding import PartitionSpec as P

BLOCK = 64
LANES = 128
HALO = 4
UNROLL = 16
ROOT = math.sqrt(math.log2(math.e))
STEP = 0.5
GAMMA = 0.5
mass_values = (1.0, 0.3, 2.5, 0.75)
strength_values = (1.0, 0.5, 1.5, 0.8)
reach_values = (1.0, 0.6, 1.4, 0.9)
MESH = pl.DeviceIdType.MESH
highest = lax.Precision.HIGHEST


def lookup(values, species):
    out = jnp.full(species.shape, values[3], jnp.float32)
    for k in range(3):
        out = jnp.where(species == k, values[k], out)
    return out


def modes_matrix(n):
    j = np.arange(n)[:, None]
    k = np.arange(n)[None, :]
    phase = 2 * np.pi * (j * k % n) / n
    m = np.where(k < n // 2, np.cos(phase), np.sin(phase)) * math.sqrt(2.0 / n)
    m = np.where(k == 0, math.sqrt(1.0 / n), m)
    m = np.where(k == n // 2, np.where(j % 2 == 0, 1, -1) * math.sqrt(1.0 / n), m)
    return m.astype(np.float32)


def mode_factors(n):
    k = np.arange(n)
    omega = 2 * np.sin(np.pi * k / n)
    gamma = np.where(k == 0, GAMMA, 2 * omega)
    c1 = np.exp(-gamma * STEP)
    c2 = np.sqrt(1 - c1 * c1)
    safe = np.where(k == 0, 1.0, omega)
    drift = np.where(k == 0, STEP, np.sin(omega * STEP) / safe)
    pull = omega * np.sin(omega * STEP)
    turn = np.cos(omega * STEP)
    out = np.zeros((n, LANES), np.float32)
    for c, v in enumerate((c1, c2, turn, drift, pull)):
        out[:, c] = v
    return out


def exchange_kernel(pos_hbm, mom_hbm, frc_hbm, noise_hbm, sp_ref, halo_ref, cos_ref, cost_ref, fac_ref,
                    pm_hbm, lo_hbm, up_hbm, hlo_ref, hup_ref,
                    raw, out_buf, in_buf, back_buf, pm_ref, load, store, send1, recv1, send2, recv2, nsend, nrecv):
    beads = lax.axis_size("bead")
    me = lax.axis_index("bead")
    shard = lax.axis_index("space")
    shards = lax.axis_size("space")
    has_lower = shard > 0
    has_upper = shard < shards - 1

    loads = [pltpu.make_async_copy(src, raw.at[n], load.at[n])
             for n, src in enumerate((pos_hbm, mom_hbm, frc_hbm, noise_hbm))]
    for c in loads:
        c.start()

    barrier = pltpu.get_barrier_semaphore()

    def each(body, unroll=4):
        def run(d, _):
            body(d)
            return 0
        lax.fori_loop(1, beads, run, 0, unroll=unroll)

    each(lambda d: pl.semaphore_signal(
        barrier, inc=1, device_id={"bead": lax.rem(me + d, beads)}, device_id_type=MESH))

    @pl.when(has_lower)
    def _():
        pl.semaphore_signal(barrier, inc=1, device_id={"space": shard - 1}, device_id_type=MESH)

    @pl.when(has_upper)
    def _():
        pl.semaphore_signal(barrier, inc=1, device_id={"space": shard + 1}, device_id_type=MESH)

    for c in loads:
        c.wait()
    for c in range(3):
        s = slice(beads * c, beads * (c + 1))
        out_buf[pl.ds(c, beads, stride=9), :] = raw[0, s]
        out_buf[pl.ds(3 + c, beads, stride=9), :] = raw[1, s] + (0.5 * STEP) * raw[2, s]
        out_buf[pl.ds(6 + c, beads, stride=9), :] = raw[3, s]
    kinds = sp_ref[...]
    pm_ref[:, 6, :] = lookup(reach_values, kinds)
    pm_ref[:, 7, :] = lookup(strength_values, kinds)

    pl.semaphore_wait(barrier, beads - 1 + has_lower.astype(jnp.int32) + has_upper.astype(jnp.int32))

    def first(d):
        j = lax.rem(me + d, beads)
        return pltpu.make_async_remote_copy(
            src_ref=out_buf.at[pl.ds(9 * j, 9)], dst_ref=in_buf.at[pl.ds(9 * me, 9)], send_sem=send1, recv_sem=recv1,
            device_id={"bead": j}, device_id_type=MESH)

    def second(d):
        j = lax.rem(me + d, beads)
        return pltpu.make_async_remote_copy(
            src_ref=back_buf.at[j, 0:6], dst_ref=pm_ref.at[me, 0:6], send_sem=send2, recv_sem=recv2,
            device_id={"bead": j}, device_id_type=MESH)

    def all_of(buf, rows, sem):
        part = buf.at[0:beads - 1, 0:rows]
        pltpu.make_async_copy(part, part, sem).wait()

    def all_rows(buf, rows, sem):
        part = buf.at[0:rows * (beads - 1)]
        pltpu.make_async_copy(part, part, sem).wait()

    def towards(up, n):
        src, dst = ((halo_ref, hlo_ref if up else hup_ref),
                    (pm_ref.at[:, 3:8], (lo_hbm if up else up_hbm).at[:, 3:8]))[n]
        k = 2 * int(up) + n
        return pltpu.make_async_remote_copy(
            src_ref=src, dst_ref=dst, send_sem=nsend.at[k], recv_sem=nrecv.at[k],
            device_id={"space": shard + 1 if up else shard - 1}, device_id_type=MESH)

    def beside(n, act, receiving=False):
        for up, there in ((True, has_upper), (False, has_lower)):
            if receiving:
                there = has_lower if up else has_upper

            @pl.when(there)
            def _(up=up):
                act(towards(up, n))

    each(lambda d: first(d).start())
    beside(0, lambda c: c.start())
    in_buf[pl.ds(9 * me, 9), :] = out_buf[pl.ds(9 * me, 9), :]
    all_rows(in_buf, 9, recv1)

    x = jnp.concatenate([in_buf[pl.ds(r, beads, stride=9), :] for r in range(6)], axis=1)
    xi = jnp.concatenate([in_buf[pl.ds(r, beads, stride=9), :] for r in range(6, 9)], axis=1)
    modes = jnp.dot(cost_ref[...], x, precision=highest, preferred_element_type=jnp.float32)
    q, p = modes[:, 0:3 * LANES], modes[:, 3 * LANES:]
    mass = lookup(mass_values, sp_ref[pl.ds(me, 1), :])
    mass3 = jnp.concatenate([mass] * 3, axis=1)
    c1, c2, turn, drift, pull = (fac_ref[:, c:c + 1] for c in range(5))
    mixed = c1 * p + c2 * (jnp.sqrt(mass3) * xi)
    q_next = turn * q + drift * (mixed / mass3)
    p_next = turn * mixed - pull * (mass3 * q)
    beads_out = jnp.dot(cos_ref[...], jnp.concatenate([p_next, q_next], axis=1), precision=highest,
                        preferred_element_type=jnp.float32)
    for r in range(6):
        back_buf[:, r, :] = beads_out[:, LANES * r:LANES * (r + 1)]

    each(lambda d: second(d).start())
    pm_ref[me, 0:6] = back_buf[me, 0:6]
    all_of(pm_ref, 6, recv2)

    keep = pltpu.make_async_copy(pm_ref, pm_hbm, store.at[0])
    keep.start()
    beside(1, lambda c: c.start())
    all_rows(out_buf, 9, send1)
    beside(0, lambda c: c.wait_send())
    beside(0, lambda c: c.wait_recv(), True)
    all_of(back_buf, 6, send2)
    beside(1, lambda c: c.wait_send())
    beside(1, lambda c: c.wait_recv(), True)
    keep.wait()


def exchange(pos, mom, frc, noise, species, halo):
    beads = lax.axis_size("bead")
    chunks = species.shape[0]
    vmem = pl.BlockSpec(memory_space=pltpu.VMEM)
    hbm = pl.BlockSpec(memory_space=pl.ANY)
    f32 = jnp.float32
    block = jax.ShapeDtypeStruct((chunks, 8, LANES), f32)
    ids = jax.ShapeDtypeStruct(halo.shape, jnp.int32)
    dma = pltpu.SemaphoreType.DMA
    matrix = modes_matrix(beads)
    return pl.pallas_call(
        exchange_kernel,
        out_shape=(block, block, block, ids, ids),
        in_specs=[hbm] * 4 + [vmem] * 5,
        out_specs=(hbm,) * 3 + (vmem,) * 2,
        scratch_shapes=[
            pltpu.VMEM((4, 3 * chunks, LANES), f32),
            pltpu.VMEM((beads * 9, LANES), f32),
            pltpu.VMEM((beads * 9, LANES), f32),
            pltpu.VMEM((beads, 8, LANES), f32),
            pltpu.VMEM((chunks, 8, LANES), f32),
            dma((4,)), dma((1,)), dma, dma, dma, dma, dma((4,)), dma((4,)),
        ],
        compiler_params=pltpu.CompilerParams(collective_id=0, has_side_effects=True),
        name="exchange",
    )(pos, mom, frc, noise, species, halo, jnp.asarray(matrix), jnp.asarray(matrix.T), jnp.asarray(mode_factors(beads)))


def force_kernel(pairs_ref, count_ref, hlo_ref, hup_ref, pm_hbm, lo_hbm, up_hbm, pos_ref, mom_ref, frc_ref,
                 tab_j, tab_i, acc, pm_ref, halo, sem):
    chunks = pm_ref.shape[0]
    blocks = 2 * chunks
    left = lax.broadcasted_iota(jnp.int32, (32, LANES), 1) < 64
    left1 = left[0:8]
    get_own = pltpu.make_async_copy(pm_hbm, pm_ref, sem.at[0])
    get_own.start()
    sides = []
    shard = lax.axis_index("space")
    for side in range(2):
        there = shard > 0 if side == 0 else shard < lax.axis_size("space") - 1
        for h in range(HALO):
            b = jnp.where(there, (hup_ref if side else hlo_ref)[1 - side, h], 0)
            get = pltpu.make_async_copy((up_hbm if side else lo_hbm).at[b // 2], halo.at[side * HALO + h], sem.at[1 + side * HALO + h])
            get.start()
            sides.append((get, there, b % 2))

    def clear(i, _):
        acc[i] = jnp.zeros((24, LANES), jnp.float32)
        return 0
    lax.fori_loop(0, blocks, clear, 0, unroll=8)
    tab_j[2 * HALO + blocks] = jnp.zeros(tab_j.shape[1:], jnp.float32)

    row = lax.broadcasted_iota(jnp.int32, (32, LANES), 0)
    lane = lax.broadcasted_iota(jnp.int32, (32, LANES), 1)
    picks = [(lane == 64 * h + row) | (lane == 64 * h + 32 + row) for h in range(2)]
    k = lax.broadcasted_iota(jnp.int32, (2 * LANES, LANES), 0)
    n = lax.broadcasted_iota(jnp.int32, (2 * LANES, LANES), 1)
    halves = ((k % 64 < 32) == (n < 64)).astype(jnp.bfloat16)
    kind = lax.broadcasted_iota(jnp.int32, (8, LANES), 0)
    factor = jnp.where(kind < 3, 1.0, jnp.where(kind < 6, ROOT, jnp.where(kind == 6, -1.0, 1.0)))

    def parts(m8):
        high = m8.astype(jnp.bfloat16).astype(jnp.float32)
        rest = m8 - high
        mid = rest.astype(jnp.bfloat16).astype(jnp.float32)
        return high, mid, rest - mid

    def spread_mxu(m8, hs):
        ps = parts(m8)
        lhs = [jnp.concatenate([jnp.where(picks[h], p[3 + c:4 + c], 0.0) for h in hs for c in range(5)], axis=0).astype(jnp.bfloat16) for p in ps]
        both = jnp.concatenate([lhs[0], lhs[1]], axis=1)
        out = jnp.dot(both, halves, preferred_element_type=jnp.float32)
        return out + jnp.dot(lhs[2], halves[0:LANES], preferred_element_type=jnp.float32)

    get_own.wait()

    def own(t, _):
        m8 = pm_ref[t] * factor
        out = spread_mxu(m8, (0, 1))
        for h in range(2):
            for c in range(5):
                s = 160 * h + 32 * c
                tab_j[HALO + 2 * t + h, c] = out[s:s + 32]
        turned = pltpu.roll(m8, 64, 1)
        for h in range(2):
            both = jnp.where(left1, m8, turned) if h == 0 else jnp.where(left1, turned, m8)
            for c in range(4):
                tab_i[2 * t + h, c] = jnp.broadcast_to(both[3 + c:4 + c], (8, LANES))
        return 0
    lax.fori_loop(0, chunks, own, 0, unroll=8)

    for get, _, _ in sides:
        get.wait()
    for n_, (get, there, half) in enumerate(sides):
        e = n_ if n_ < HALO else blocks + n_
        m8 = jnp.where(there, halo[n_], 0.0) * factor
        m8 = jnp.where(half == 1, pltpu.roll(m8, 64, 1), m8)
        out = spread_mxu(m8, (0,))
        for c in range(5):
            tab_j[e, c] = out[32 * c:32 * c + 32]

    live = count_ref[0]

    def pair(p):
        i = pairs_ref[0, p]
        j = jnp.where(p < live, pairs_ref[1, p], 2 * HALO + blocks)
        xi, yi, zi, ri = (tab_i[i, c] for c in range(4))
        f = [None] * 3
        for g in range(4):
            s = pl.ds(8 * g, 8)
            dx = xi - tab_j[j, 0, s]
            dy = yi - tab_j[j, 1, s]
            dz = zi - tab_j[j, 2, s]
            d = dx * dx + dy * dy + dz * dz
            inv = 1.0 / (ri + tab_j[j, 3, s])
            w = jnp.exp2(d * inv) * (inv * tab_j[j, 4, s])
            for k, v in enumerate((dx, dy, dz)):
                f[k] = w * v if g == 0 else f[k] + w * v
        return i, f

    def group(g, _):
        for u in range(UNROLL):
            i, f = pair(g * UNROLL + u)
            for k in range(3):
                acc[i, pl.ds(8 * k, 8)] = acc[i, pl.ds(8 * k, 8)] + f[k]
        return 0
    lax.fori_loop(0, (live + UNROLL - 1) // UNROLL, group, 0)

    def finish(t, _):
        rows = pm_ref[t]
        scale = (-0.02 / ROOT) * rows[7:8]
        for k in range(3):
            v = [jnp.sum(acc[2 * t + h, pl.ds(8 * k, 8)], axis=0, keepdims=True) for h in range(2)]
            v = [x + pltpu.roll(x, 64, 1) for x in v]
            f = jnp.where(left[0:1], v[0], v[1]) * scale
            at = pl.ds(k * chunks + t, 1)
            pos_ref[at, :] = rows[3 + k:4 + k]
            frc_ref[at, :] = f
            mom_ref[at, :] = rows[k:k + 1] + 0.25 * f
        return 0
    lax.fori_loop(0, chunks, finish, 0, unroll=8)


def force_call(pairs, count, hlo, hup, pm, lo, up):
    chunks = pm.shape[0]
    smem = pl.BlockSpec(memory_space=pltpu.SMEM)
    vmem = pl.BlockSpec(memory_space=pltpu.VMEM)
    hbm = pl.BlockSpec(memory_space=pl.ANY)
    o = jax.ShapeDtypeStruct((3 * chunks, LANES), jnp.float32)
    return pl.pallas_call(
        force_kernel,
        out_shape=(o, o, o),
        in_specs=[smem] * 4 + [hbm] * 3,
        out_specs=(vmem,) * 3,
        scratch_shapes=[
            pltpu.VMEM((2 * chunks + 2 * HALO + 1, 5, 32, LANES), jnp.float32),
            pltpu.VMEM((2 * chunks, 4, 8, LANES), jnp.float32),
            pltpu.VMEM((2 * chunks, 24, LANES), jnp.float32),
            pltpu.VMEM((chunks, 8, LANES), jnp.float32),
            pltpu.VMEM((2 * HALO, 8, LANES), jnp.float32),
            pltpu.SemaphoreType.DMA((1 + 2 * HALO,)),
        ],
        compiler_params=pltpu.CompilerParams(vmem_limit_bytes=60 * 2**20),
        name="pair_forces",
    )(pairs, count, hlo, hup, pm, lo, up)


def shards(positions, momenta, forces, noise, species, block_pairs, pair_count, halo_blocks):
    flat = [a.reshape(-1, LANES) for a in (positions, momenta, forces, noise)]
    pm, lo, up, hlo, hup = exchange(*flat, species.reshape(-1, LANES), halo_blocks)
    outs = force_call(block_pairs, pair_count, hlo, hup, pm, lo, up)
    return tuple(o.reshape(positions.shape) for o in outs)


def solution(mesh):
    big = P("bead", None, "space")
    in_specs = (big, big, big, big, P("space"), P(None, "space"), P("space"), P(None, "space"))
    return jax.shard_map(shards, mesh=mesh, in_specs=in_specs, out_specs=(big, big, big), check_vma=False)
```

```python
import functools
import math

import jax
import jax.numpy as jnp
import numpy as np
from jax import lax
from jax.experimental import pallas as pl
from jax.experimental.pallas import tpu as pltpu
from jax.sharding import PartitionSpec as P

BLOCK = 64
LANES = 128
HALO = 4
UNROLL = 64
ROOT = math.sqrt(math.log2(math.e))
STEP = 0.5
GAMMA = 0.5
mass_values = (1.0, 0.3, 2.5, 0.75)
strength_values = (1.0, 0.5, 1.5, 0.8)
reach_values = (1.0, 0.6, 1.4, 0.9)
MESH = pl.DeviceIdType.MESH
highest = lax.Precision.HIGHEST


def lookup(values, species):
    out = jnp.full(species.shape, values[3], jnp.float32)
    for k in range(3):
        out = jnp.where(species == k, values[k], out)
    return out


def modes_matrix(n):
    j = np.arange(n)[:, None]
    k = np.arange(n)[None, :]
    phase = 2 * np.pi * (j * k % n) / n
    m = np.where(k < n // 2, np.cos(phase), np.sin(phase)) * math.sqrt(2.0 / n)
    m = np.where(k == 0, math.sqrt(1.0 / n), m)
    m = np.where(k == n // 2, np.where(j % 2 == 0, 1, -1) * math.sqrt(1.0 / n), m)
    return m.astype(np.float32)


def mode_factors(n):
    k = np.arange(n)
    omega = 2 * np.sin(np.pi * k / n)
    gamma = np.where(k == 0, GAMMA, 2 * omega)
    c1 = np.exp(-gamma * STEP)
    c2 = np.sqrt(1 - c1 * c1)
    safe = np.where(k == 0, 1.0, omega)
    drift = np.where(k == 0, STEP, np.sin(omega * STEP) / safe)
    pull = omega * np.sin(omega * STEP)
    turn = np.cos(omega * STEP)
    out = np.zeros((n, LANES), np.float32)
    for c, v in enumerate((c1, c2, turn, drift, pull)):
        out[:, c] = v
    return out


def exchange_kernel(pos_hbm, mom_hbm, frc_hbm, noise_hbm, sp_ref, halo_ref, cos_ref, cost_ref, fac_ref,
                    pm_hbm, lo_hbm, up_hbm, hlo_ref, hup_ref,
                    raw, out_buf, in_buf, back_buf, pm_ref, load, store, send1, recv1, send2, recv2, nsend, nrecv):
    beads = lax.axis_size("bead")
    me = lax.axis_index("bead")
    shard = lax.axis_index("space")
    shards = lax.axis_size("space")
    has_lower = shard > 0
    has_upper = shard < shards - 1

    loads = [pltpu.make_async_copy(src, raw.at[n], load.at[n])
             for n, src in enumerate((pos_hbm, mom_hbm, frc_hbm, noise_hbm))]
    for c in loads:
        c.start()

    barrier = pltpu.get_barrier_semaphore()

    def each(body, first=1, unroll=4):
        def run(d, _):
            body(d)
            return 0
        lax.fori_loop(first, beads, run, 0, unroll=unroll)

    each(lambda d: pl.semaphore_signal(
        barrier, inc=1, device_id={"bead": lax.rem(me + d, beads)}, device_id_type=MESH))

    for there, other in ((has_lower, shard - 1), (has_upper, shard + 1)):
        @pl.when(there)
        def _(other=other):
            each(lambda d: pl.semaphore_signal(
                barrier, inc=1, device_id={"bead": lax.rem(me + d, beads), "space": other}, device_id_type=MESH), 0)

    for c in loads:
        c.wait()
    for c in range(3):
        s = slice(beads * c, beads * (c + 1))
        out_buf[pl.ds(c, beads, stride=9), :] = raw[0, s]
        out_buf[pl.ds(3 + c, beads, stride=9), :] = raw[1, s] + (0.5 * STEP) * raw[2, s]
        out_buf[pl.ds(6 + c, beads, stride=9), :] = raw[3, s]
    kinds = sp_ref[...]
    pm_ref[:, 6, :] = lookup(reach_values, kinds)
    pm_ref[:, 7, :] = lookup(strength_values, kinds)

    pl.semaphore_wait(barrier, beads - 1 + beads * (has_lower.astype(jnp.int32) + has_upper.astype(jnp.int32)))

    def first(d):
        j = lax.rem(me + d, beads)
        return pltpu.make_async_remote_copy(
            src_ref=out_buf.at[pl.ds(9 * j, 9)], dst_ref=in_buf.at[pl.ds(9 * me, 9)], send_sem=send1, recv_sem=recv1,
            device_id={"bead": j}, device_id_type=MESH)

    def second(d):
        j = lax.rem(me + d, beads)
        return pltpu.make_async_remote_copy(
            src_ref=back_buf.at[j, 0:6], dst_ref=pm_ref.at[me, 0:6], send_sem=send2, recv_sem=recv2,
            device_id={"bead": j}, device_id_type=MESH)

    def all_of(buf, rows, sem):
        part = buf.at[0:beads - 1, 0:rows]
        pltpu.make_async_copy(part, part, sem).wait()

    def all_rows(buf, rows, sem):
        part = buf.at[0:rows * (beads - 1)]
        pltpu.make_async_copy(part, part, sem).wait()

    def lists(up):
        return pltpu.make_async_remote_copy(
            src_ref=halo_ref, dst_ref=hlo_ref if up else hup_ref, send_sem=nsend.at[int(up)],
            recv_sem=nrecv.at[int(up)], device_id={"space": shard + 1 if up else shard - 1}, device_id_type=MESH)

    def bounds(up):
        return pltpu.make_async_remote_copy(
            src_ref=pm_ref.at[:, 6:8], dst_ref=(lo_hbm if up else up_hbm).at[:, 6:8], send_sem=nsend.at[4 + int(up)],
            recv_sem=nrecv.at[4 + int(up)], device_id={"space": shard + 1 if up else shard - 1}, device_id_type=MESH)

    def beyond(up, d):
        j = lax.rem(me + d, beads)
        return pltpu.make_async_remote_copy(
            src_ref=back_buf.at[j, 3:6], dst_ref=(lo_hbm if up else up_hbm).at[me, 3:6],
            send_sem=nsend.at[2 + int(up)], recv_sem=nrecv.at[2 + int(up)],
            device_id={"bead": j, "space": shard + 1 if up else shard - 1}, device_id_type=MESH)

    def beside(act, receiving=False):
        for up, there in ((True, has_upper), (False, has_lower)):
            if receiving:
                there = has_lower if up else has_upper

            @pl.when(there)
            def _(up=up):
                act(up)

    def all_beyond(buf, sem):
        part = buf.at[:, 3:6]
        pltpu.make_async_copy(part, part, sem).wait()

    each(lambda d: first(d).start())
    beside(lambda up: (lists(up).start(), bounds(up).start()))
    in_buf[pl.ds(9 * me, 9), :] = out_buf[pl.ds(9 * me, 9), :]
    all_rows(in_buf, 9, recv1)

    x = jnp.concatenate([in_buf[pl.ds(r, beads, stride=9), :] for r in range(6)], axis=1)
    xi = jnp.concatenate([in_buf[pl.ds(r, beads, stride=9), :] for r in range(6, 9)], axis=1)
    modes = jnp.dot(cost_ref[...], x, precision=highest, preferred_element_type=jnp.float32)
    q, p = modes[:, 0:3 * LANES], modes[:, 3 * LANES:]
    mass = lookup(mass_values, sp_ref[pl.ds(me, 1), :])
    mass3 = jnp.concatenate([mass] * 3, axis=1)
    c1, c2, turn, drift, pull = (fac_ref[:, c:c + 1] for c in range(5))
    mixed = c1 * p + c2 * (jnp.sqrt(mass3) * xi)
    q_next = turn * q + drift * (mixed / mass3)
    p_next = turn * mixed - pull * (mass3 * q)
    beads_out = jnp.dot(cos_ref[...], jnp.concatenate([p_next, q_next], axis=1), precision=highest,
                        preferred_element_type=jnp.float32)
    for r in range(6):
        back_buf[:, r, :] = beads_out[:, LANES * r:LANES * (r + 1)]

    each(lambda d: second(d).start())
    beside(lambda up: each(lambda d: beyond(up, d).start(), 0))
    pm_ref[me, 0:6] = back_buf[me, 0:6]
    all_of(pm_ref, 6, recv2)

    keep = pltpu.make_async_copy(pm_ref, pm_hbm, store.at[0])
    keep.start()
    all_rows(out_buf, 9, send1)
    beside(lambda up: (lists(up).wait_send(), bounds(up).wait_send()))
    beside(lambda up: (lists(up).wait_recv(), bounds(up).wait_recv()), True)
    all_of(back_buf, 6, send2)
    beside(lambda up: all_beyond(back_buf, nsend.at[2 + int(up)]))
    beside(lambda up: all_beyond(lo_hbm if up else up_hbm, nrecv.at[2 + int(up)]), True)
    keep.wait()


def exchange(pos, mom, frc, noise, species, halo):
    beads = lax.axis_size("bead")
    chunks = species.shape[0]
    vmem = pl.BlockSpec(memory_space=pltpu.VMEM)
    hbm = pl.BlockSpec(memory_space=pl.ANY)
    f32 = jnp.float32
    block = jax.ShapeDtypeStruct((chunks, 8, LANES), f32)
    ids = jax.ShapeDtypeStruct(halo.shape, jnp.int32)
    dma = pltpu.SemaphoreType.DMA
    matrix = modes_matrix(beads)
    return pl.pallas_call(
        exchange_kernel,
        out_shape=(block, block, block, ids, ids),
        in_specs=[hbm] * 4 + [vmem] * 5,
        out_specs=(hbm,) * 3 + (vmem,) * 2,
        scratch_shapes=[
            pltpu.VMEM((4, 3 * chunks, LANES), f32),
            pltpu.VMEM((beads * 9, LANES), f32),
            pltpu.VMEM((beads * 9, LANES), f32),
            pltpu.VMEM((beads, 8, LANES), f32),
            pltpu.VMEM((chunks, 8, LANES), f32),
            dma((4,)), dma((1,)), dma, dma, dma, dma, dma((6,)), dma((6,)),
        ],
        compiler_params=pltpu.CompilerParams(collective_id=0, has_side_effects=True),
        name="exchange",
    )(pos, mom, frc, noise, species, halo, jnp.asarray(matrix), jnp.asarray(matrix.T), jnp.asarray(mode_factors(beads)))


def force_kernel(pairs_ref, count_ref, hlo_ref, hup_ref, pm_hbm, lo_hbm, up_hbm, pos_ref, mom_ref, frc_ref,
                 tab_j, tab_i, acc, pm_ref, halo, sem):
    chunks = pm_ref.shape[0]
    blocks = 2 * chunks
    left = lax.broadcasted_iota(jnp.int32, (32, LANES), 1) < 64
    left1 = left[0:8]
    get_own = pltpu.make_async_copy(pm_hbm, pm_ref, sem.at[0])
    get_own.start()
    sides = []
    shard = lax.axis_index("space")
    for side in range(2):
        there = shard > 0 if side == 0 else shard < lax.axis_size("space") - 1
        for h in range(HALO):
            b = jnp.where(there, (hup_ref if side else hlo_ref)[1 - side, h], 0)
            get = pltpu.make_async_copy((up_hbm if side else lo_hbm).at[b // 2], halo.at[side * HALO + h], sem.at[1 + side * HALO + h])
            get.start()
            sides.append((get, there, b % 2))

    def clear(i, _):
        acc[i] = jnp.zeros((24, LANES), jnp.float32)
        return 0
    lax.fori_loop(0, blocks, clear, 0, unroll=8)
    tab_j[2 * HALO + blocks] = jnp.zeros(tab_j.shape[1:], jnp.float32)

    row = lax.broadcasted_iota(jnp.int32, (32, LANES), 0)
    lane = lax.broadcasted_iota(jnp.int32, (32, LANES), 1)
    picks = [(lane == 64 * h + row) | (lane == 64 * h + 32 + row) for h in range(2)]
    k = lax.broadcasted_iota(jnp.int32, (2 * LANES, LANES), 0)
    n = lax.broadcasted_iota(jnp.int32, (2 * LANES, LANES), 1)
    halves = ((k % 64 < 32) == (n < 64)).astype(jnp.bfloat16)
    kind = lax.broadcasted_iota(jnp.int32, (8, LANES), 0)
    factor = jnp.where(kind < 3, 1.0, jnp.where(kind < 6, ROOT, jnp.where(kind == 6, -1.0, 1.0)))

    def parts(m8):
        high = m8.astype(jnp.bfloat16).astype(jnp.float32)
        rest = m8 - high
        mid = rest.astype(jnp.bfloat16).astype(jnp.float32)
        return high, mid, rest - mid

    def spread_mxu(m8, hs):
        ps = parts(m8)
        lhs = [jnp.concatenate([jnp.where(picks[h], p[3 + c:4 + c], 0.0) for h in hs for c in range(5)], axis=0).astype(jnp.bfloat16) for p in ps]
        both = jnp.concatenate([lhs[0], lhs[1]], axis=1)
        out = jnp.dot(both, halves, preferred_element_type=jnp.float32)
        return out + jnp.dot(lhs[2], halves[0:LANES], preferred_element_type=jnp.float32)

    get_own.wait()

    def own(t, _):
        m8 = pm_ref[t] * factor
        out = spread_mxu(m8, (0, 1))
        for h in range(2):
            for c in range(5):
                s = 160 * h + 32 * c
                tab_j[HALO + 2 * t + h, c] = out[s:s + 32]
        turned = pltpu.roll(m8, 64, 1)
        for h in range(2):
            both = jnp.where(left1, m8, turned) if h == 0 else jnp.where(left1, turned, m8)
            for c in range(4):
                tab_i[2 * t + h, c] = jnp.broadcast_to(both[3 + c:4 + c], (8, LANES))
        return 0
    lax.fori_loop(0, chunks, own, 0, unroll=16)

    for get, _, _ in sides:
        get.wait()
    for n_, (get, there, half) in enumerate(sides):
        e = n_ if n_ < HALO else blocks + n_
        m8 = jnp.where(there, halo[n_], 0.0) * factor
        m8 = jnp.where(half == 1, pltpu.roll(m8, 64, 1), m8)
        out = spread_mxu(m8, (0,))
        for c in range(5):
            tab_j[e, c] = out[32 * c:32 * c + 32]

    live = count_ref[0]

    def pair(p):
        i = pairs_ref[0, p]
        j = jnp.where(p < live, pairs_ref[1, p], 2 * HALO + blocks)
        xi, yi, zi, ri = (tab_i[i, c] for c in range(4))
        f = [None] * 3
        for g in range(4):
            s = pl.ds(8 * g, 8)
            dx = xi - tab_j[j, 0, s]
            dy = yi - tab_j[j, 1, s]
            dz = zi - tab_j[j, 2, s]
            d = dx * dx + dy * dy + dz * dz
            inv = 1.0 / (ri + tab_j[j, 3, s])
            w = jnp.exp2(d * inv) * (inv * tab_j[j, 4, s])
            for k, v in enumerate((dx, dy, dz)):
                f[k] = w * v if g == 0 else f[k] + w * v
        return i, f

    def group(g, _):
        for u in range(UNROLL):
            i, f = pair(g * UNROLL + u)
            for k in range(3):
                acc[i, pl.ds(8 * k, 8)] = acc[i, pl.ds(8 * k, 8)] + f[k]
        return 0
    lax.fori_loop(0, (live + UNROLL - 1) // UNROLL, group, 0)

    def finish(t, _):
        rows = pm_ref[t]
        scale = (-0.02 / ROOT) * rows[7:8]
        for k in range(3):
            v = [jnp.sum(acc[2 * t + h, pl.ds(8 * k, 8)], axis=0, keepdims=True) for h in range(2)]
            v = [x + pltpu.roll(x, 64, 1) for x in v]
            f = jnp.where(left[0:1], v[0], v[1]) * scale
            at = pl.ds(k * chunks + t, 1)
            pos_ref[at, :] = rows[3 + k:4 + k]
            frc_ref[at, :] = f
            mom_ref[at, :] = rows[k:k + 1] + 0.25 * f
        return 0
    lax.fori_loop(0, chunks, finish, 0, unroll=8)


def force_call(pairs, count, hlo, hup, pm, lo, up):
    chunks = pm.shape[0]
    smem = pl.BlockSpec(memory_space=pltpu.SMEM)
    vmem = pl.BlockSpec(memory_space=pltpu.VMEM)
    hbm = pl.BlockSpec(memory_space=pl.ANY)
    o = jax.ShapeDtypeStruct((3 * chunks, LANES), jnp.float32)
    return pl.pallas_call(
        force_kernel,
        out_shape=(o, o, o),
        in_specs=[smem] * 4 + [hbm] * 3,
        out_specs=(vmem,) * 3,
        scratch_shapes=[
            pltpu.VMEM((2 * chunks + 2 * HALO + 1, 5, 32, LANES), jnp.float32),
            pltpu.VMEM((2 * chunks, 4, 8, LANES), jnp.float32),
            pltpu.VMEM((2 * chunks, 24, LANES), jnp.float32),
            pltpu.VMEM((chunks, 8, LANES), jnp.float32),
            pltpu.VMEM((2 * HALO, 8, LANES), jnp.float32),
            pltpu.SemaphoreType.DMA((1 + 2 * HALO,)),
        ],
        compiler_params=pltpu.CompilerParams(vmem_limit_bytes=60 * 2**20),
        name="pair_forces",
    )(pairs, count, hlo, hup, pm, lo, up)


def shards(positions, momenta, forces, noise, species, block_pairs, pair_count, halo_blocks):
    flat = [a.reshape(-1, LANES) for a in (positions, momenta, forces, noise)]
    pm, lo, up, hlo, hup = exchange(*flat, species.reshape(-1, LANES), halo_blocks)
    outs = force_call(block_pairs, pair_count, hlo, hup, pm, lo, up)
    return tuple(o.reshape(positions.shape) for o in outs)


def solution(mesh):
    big = P("bead", None, "space")
    in_specs = (big, big, big, big, P("space"), P(None, "space"), P("space"), P(None, "space"))
    return jax.shard_map(shards, mesh=mesh, in_specs=in_specs, out_specs=(big, big, big), check_vma=False)
```

```python
import functools
import math

import jax
import jax.numpy as jnp
import numpy as np
from jax import lax
from jax.experimental import pallas as pl
from jax.experimental.pallas import tpu as pltpu
from jax.sharding import PartitionSpec as P

BLOCK = 64
LANES = 128
HALO = 4
UNROLL = 64
ROOT = math.sqrt(math.log2(math.e))
STEP = 0.5
GAMMA = 0.5
mass_values = (1.0, 0.3, 2.5, 0.75)
strength_values = (1.0, 0.5, 1.5, 0.8)
reach_values = (1.0, 0.6, 1.4, 0.9)
MESH = pl.DeviceIdType.MESH
highest = lax.Precision.HIGHEST


def lookup(values, species):
    out = jnp.full(species.shape, values[3], jnp.float32)
    for k in range(3):
        out = jnp.where(species == k, values[k], out)
    return out


def modes_matrix(n):
    j = np.arange(n)[:, None]
    k = np.arange(n)[None, :]
    phase = 2 * np.pi * (j * k % n) / n
    m = np.where(k < n // 2, np.cos(phase), np.sin(phase)) * math.sqrt(2.0 / n)
    m = np.where(k == 0, math.sqrt(1.0 / n), m)
    m = np.where(k == n // 2, np.where(j % 2 == 0, 1, -1) * math.sqrt(1.0 / n), m)
    return m.astype(np.float32)


def mode_factors(n):
    k = np.arange(n)
    omega = 2 * np.sin(np.pi * k / n)
    gamma = np.where(k == 0, GAMMA, 2 * omega)
    c1 = np.exp(-gamma * STEP)
    c2 = np.sqrt(1 - c1 * c1)
    safe = np.where(k == 0, 1.0, omega)
    drift = np.where(k == 0, STEP, np.sin(omega * STEP) / safe)
    pull = omega * np.sin(omega * STEP)
    turn = np.cos(omega * STEP)
    out = np.zeros((n, LANES), np.float32)
    for c, v in enumerate((c1, c2, turn, drift, pull)):
        out[:, c] = v
    return out


def exchange_kernel(pos_hbm, mom_hbm, frc_hbm, noise_hbm, sp_hbm, halo_hbm, fixed_hbm,
                    pm_hbm, lo_hbm, up_hbm, hlo_hbm, hup_hbm,
                    raw, sp_ref, fixed, out_buf, in_buf, back_buf, range_buf, load, store, send1, recv1, send2, recv2, nsend, nrecv):
    beads = lax.axis_size("bead")
    me = lax.axis_index("bead")
    shard = lax.axis_index("space")
    shards = lax.axis_size("space")
    has_lower = shard > 0
    has_upper = shard < shards - 1

    barrier = pltpu.get_barrier_semaphore()

    def each(body, first=1, unroll=4):
        def run(d, _):
            body(d)
            return 0
        lax.fori_loop(first, beads, run, 0, unroll=unroll)

    each(lambda d: pl.semaphore_signal(
        barrier, inc=1, device_id={"bead": lax.rem(me + d, beads)}, device_id_type=MESH))

    for there, other in ((has_lower, shard - 1), (has_upper, shard + 1)):
        @pl.when(there)
        def _(other=other):
            each(lambda d: pl.semaphore_signal(
                barrier, inc=1, device_id={"bead": lax.rem(me + d, beads), "space": other}, device_id_type=MESH), 0)

    loads = [pltpu.make_async_copy(src, dst, load.at[n]) for n, (src, dst) in enumerate((
        (pos_hbm, raw.at[0]), (mom_hbm, raw.at[1]), (frc_hbm, raw.at[2]), (noise_hbm, raw.at[3]),
        (sp_hbm, sp_ref), (fixed_hbm, fixed)))]
    for c in loads:
        c.start()
    for c in loads:
        c.wait()
    for c in range(3):
        s = slice(beads * c, beads * (c + 1))
        out_buf[pl.ds(c, beads, stride=9), :] = raw[0, s]
        out_buf[pl.ds(3 + c, beads, stride=9), :] = raw[1, s] + (0.5 * STEP) * raw[2, s]
        out_buf[pl.ds(6 + c, beads, stride=9), :] = raw[3, s]
    kinds = sp_ref[...]
    range_buf[:, 0, :] = lookup(reach_values, kinds)
    range_buf[:, 1, :] = lookup(strength_values, kinds)
    keep = pltpu.make_async_copy(range_buf, pm_hbm.at[:, 6:8], store.at[0])
    keep.start()

    pl.semaphore_wait(barrier, beads - 1 + beads * (has_lower.astype(jnp.int32) + has_upper.astype(jnp.int32)))

    def first(d):
        j = lax.rem(me + d, beads)
        return pltpu.make_async_remote_copy(
            src_ref=out_buf.at[pl.ds(9 * j, 9)], dst_ref=in_buf.at[pl.ds(9 * me, 9)], send_sem=send1, recv_sem=recv1,
            device_id={"bead": j}, device_id_type=MESH)

    def second(d):
        j = lax.rem(me + d, beads)
        return pltpu.make_async_remote_copy(
            src_ref=back_buf.at[j, 0:6], dst_ref=pm_hbm.at[me, 0:6], send_sem=send2, recv_sem=recv2,
            device_id={"bead": j}, device_id_type=MESH)

    def all_of(buf, rows, sem):
        part = buf.at[0:beads - 1, 0:rows]
        pltpu.make_async_copy(part, part, sem).wait()

    def all_rows(buf, rows, sem):
        part = buf.at[0:rows * (beads - 1)]
        pltpu.make_async_copy(part, part, sem).wait()

    def lists(up):
        return pltpu.make_async_remote_copy(
            src_ref=halo_hbm, dst_ref=hlo_hbm if up else hup_hbm, send_sem=nsend.at[int(up)],
            recv_sem=nrecv.at[int(up)], device_id={"space": shard + 1 if up else shard - 1}, device_id_type=MESH)

    def bounds(up):
        return pltpu.make_async_remote_copy(
            src_ref=range_buf, dst_ref=(lo_hbm if up else up_hbm).at[:, 6:8], send_sem=nsend.at[4 + int(up)],
            recv_sem=nrecv.at[4 + int(up)], device_id={"space": shard + 1 if up else shard - 1}, device_id_type=MESH)

    def beyond(up, d):
        j = lax.rem(me + d, beads)
        return pltpu.make_async_remote_copy(
            src_ref=back_buf.at[j, 3:6], dst_ref=(lo_hbm if up else up_hbm).at[me, 3:6],
            send_sem=nsend.at[2 + int(up)], recv_sem=nrecv.at[2 + int(up)],
            device_id={"bead": j, "space": shard + 1 if up else shard - 1}, device_id_type=MESH)

    def beside(act, receiving=False):
        for up, there in ((True, has_upper), (False, has_lower)):
            if receiving:
                there = has_lower if up else has_upper

            @pl.when(there)
            def _(up=up):
                act(up)

    def all_beyond(buf, sem):
        part = buf.at[:, 3:6]
        pltpu.make_async_copy(part, part, sem).wait()

    each(lambda d: first(d).start())
    beside(lambda up: (lists(up).start(), bounds(up).start()))
    in_buf[pl.ds(9 * me, 9), :] = out_buf[pl.ds(9 * me, 9), :]
    all_rows(in_buf, 9, recv1)

    x = jnp.concatenate([in_buf[pl.ds(r, beads, stride=9), :] for r in range(6)], axis=1)
    xi = jnp.concatenate([in_buf[pl.ds(r, beads, stride=9), :] for r in range(6, 9)], axis=1)
    modes = jnp.dot(fixed[beads:2 * beads, 0:beads], x, precision=highest, preferred_element_type=jnp.float32)
    q, p = modes[:, 0:3 * LANES], modes[:, 3 * LANES:]
    mass = lookup(mass_values, sp_ref[pl.ds(me, 1), :])
    mass3 = jnp.concatenate([mass] * 3, axis=1)
    c1, c2, turn, drift, pull = (fixed[2 * beads:3 * beads, c:c + 1] for c in range(5))
    mixed = c1 * p + c2 * (jnp.sqrt(mass3) * xi)
    q_next = turn * q + drift * (mixed / mass3)
    p_next = turn * mixed - pull * (mass3 * q)
    beads_out = jnp.dot(fixed[0:beads, 0:beads], jnp.concatenate([p_next, q_next], axis=1), precision=highest,
                        preferred_element_type=jnp.float32)
    for r in range(6):
        back_buf[:, r, :] = beads_out[:, LANES * r:LANES * (r + 1)]

    each(lambda d: second(d).start())
    beside(lambda up: each(lambda d: beyond(up, d).start(), 0))
    own = pltpu.make_async_copy(back_buf.at[me, 0:6], pm_hbm.at[me, 0:6], store.at[1])
    own.start()
    all_of(pm_hbm, 6, recv2)
    own.wait()

    all_rows(out_buf, 9, send1)
    beside(lambda up: (lists(up).wait_send(), bounds(up).wait_send()))
    beside(lambda up: (lists(up).wait_recv(), bounds(up).wait_recv()), True)
    all_of(back_buf, 6, send2)
    beside(lambda up: all_beyond(back_buf, nsend.at[2 + int(up)]))
    beside(lambda up: all_beyond(lo_hbm if up else up_hbm, nrecv.at[2 + int(up)]), True)
    keep.wait()


def exchange(pos, mom, frc, noise, species, halo):
    beads = lax.axis_size("bead")
    chunks = species.shape[0]
    hbm = pl.BlockSpec(memory_space=pl.ANY)
    f32 = jnp.float32
    block = jax.ShapeDtypeStruct((chunks, 8, LANES), f32)
    ids = jax.ShapeDtypeStruct(halo.shape, jnp.int32)
    dma = pltpu.SemaphoreType.DMA
    fixed = np.zeros((3, beads, LANES), np.float32)
    fixed[0, :, 0:beads] = modes_matrix(beads)
    fixed[1, :, 0:beads] = modes_matrix(beads).T
    fixed[2] = mode_factors(beads)
    return pl.pallas_call(
        exchange_kernel,
        out_shape=(block, block, block, ids, ids),
        in_specs=[hbm] * 7,
        out_specs=(hbm,) * 5,
        scratch_shapes=[
            pltpu.VMEM((4, 3 * chunks, LANES), f32),
            pltpu.VMEM((chunks, LANES), jnp.int32),
            pltpu.VMEM((3 * beads, LANES), f32),
            pltpu.VMEM((beads * 9, LANES), f32),
            pltpu.VMEM((beads * 9, LANES), f32),
            pltpu.VMEM((beads, 8, LANES), f32),
            pltpu.VMEM((chunks, 2, LANES), f32),
            dma((6,)), dma((2,)), dma, dma, dma, dma, dma((6,)), dma((6,)),
        ],
        compiler_params=pltpu.CompilerParams(collective_id=0, has_side_effects=True),
        name="exchange",
    )(pos, mom, frc, noise, species, halo, jnp.asarray(fixed.reshape(3 * beads, LANES)))


def force_kernel(pairs_ref, count_ref, hlo_ref, hup_ref, pm_hbm, lo_hbm, up_hbm, pos_ref, mom_ref, frc_ref,
                 tab_j, tab_i, acc, pm_ref, halo, sem):
    chunks = pm_ref.shape[0]
    blocks = 2 * chunks
    left = lax.broadcasted_iota(jnp.int32, (32, LANES), 1) < 64
    left1 = left[0:8]
    get_own = pltpu.make_async_copy(pm_hbm, pm_ref, sem.at[0])
    get_own.start()
    sides = []
    shard = lax.axis_index("space")
    for side in range(2):
        there = shard > 0 if side == 0 else shard < lax.axis_size("space") - 1
        for h in range(HALO):
            b = jnp.where(there, (hup_ref if side else hlo_ref)[1 - side, h], 0)
            get = pltpu.make_async_copy((up_hbm if side else lo_hbm).at[b // 2], halo.at[side * HALO + h], sem.at[1 + side * HALO + h])
            get.start()
            sides.append((get, there, b % 2))

    def clear(i, _):
        acc[i] = jnp.zeros((24, LANES), jnp.float32)
        return 0
    lax.fori_loop(0, blocks, clear, 0, unroll=8)
    tab_j[2 * HALO + blocks] = jnp.zeros(tab_j.shape[1:], jnp.float32)

    row = lax.broadcasted_iota(jnp.int32, (32, LANES), 0)
    lane = lax.broadcasted_iota(jnp.int32, (32, LANES), 1)
    picks = [(lane == 64 * h + row) | (lane == 64 * h + 32 + row) for h in range(2)]
    k = lax.broadcasted_iota(jnp.int32, (2 * LANES, LANES), 0)
    n = lax.broadcasted_iota(jnp.int32, (2 * LANES, LANES), 1)
    halves = ((k % 64 < 32) == (n < 64)).astype(jnp.bfloat16)
    kind = lax.broadcasted_iota(jnp.int32, (8, LANES), 0)
    factor = jnp.where(kind < 3, 1.0, jnp.where(kind < 6, ROOT, jnp.where(kind == 6, -1.0, 1.0)))

    def parts(m8):
        high = m8.astype(jnp.bfloat16).astype(jnp.float32)
        rest = m8 - high
        mid = rest.astype(jnp.bfloat16).astype(jnp.float32)
        return high, mid, rest - mid

    def spread_mxu(m8, hs):
        ps = parts(m8)
        lhs = [jnp.concatenate([jnp.where(picks[h], p[3 + c:4 + c], 0.0) for h in hs for c in range(5)], axis=0).astype(jnp.bfloat16) for p in ps]
        both = jnp.concatenate([lhs[0], lhs[1]], axis=1)
        out = jnp.dot(both, halves, preferred_element_type=jnp.float32)
        return out + jnp.dot(lhs[2], halves[0:LANES], preferred_element_type=jnp.float32)

    get_own.wait()

    def own(t, _):
        m8 = pm_ref[t] * factor
        out = spread_mxu(m8, (0, 1))
        for h in range(2):
            for c in range(5):
                s = 160 * h + 32 * c
                tab_j[HALO + 2 * t + h, c] = out[s:s + 32]
        turned = pltpu.roll(m8, 64, 1)
        for h in range(2):
            both = jnp.where(left1, m8, turned) if h == 0 else jnp.where(left1, turned, m8)
            for c in range(4):
                tab_i[2 * t + h, c] = jnp.broadcast_to(both[3 + c:4 + c], (8, LANES))
        return 0
    lax.fori_loop(0, chunks, own, 0, unroll=16)

    for get, _, _ in sides:
        get.wait()
    for n_, (get, there, half) in enumerate(sides):
        e = n_ if n_ < HALO else blocks + n_
        m8 = jnp.where(there, halo[n_], 0.0) * factor
        m8 = jnp.where(half == 1, pltpu.roll(m8, 64, 1), m8)
        out = spread_mxu(m8, (0,))
        for c in range(5):
            tab_j[e, c] = out[32 * c:32 * c + 32]

    live = count_ref[0]

    def pair(p):
        i = pairs_ref[0, p]
        j = jnp.where(p < live, pairs_ref[1, p], 2 * HALO + blocks)
        xi, yi, zi, ri = (tab_i[i, c] for c in range(4))
        f = [None] * 3
        for g in range(4):
            s = pl.ds(8 * g, 8)
            dx = xi - tab_j[j, 0, s]
            dy = yi - tab_j[j, 1, s]
            dz = zi - tab_j[j, 2, s]
            d = dx * dx + dy * dy + dz * dz
            inv = 1.0 / (ri + tab_j[j, 3, s])
            w = jnp.exp2(d * inv) * (inv * tab_j[j, 4, s])
            for k, v in enumerate((dx, dy, dz)):
                f[k] = w * v if g == 0 else f[k] + w * v
        return i, f

    def group(g, _):
        for u in range(UNROLL):
            i, f = pair(g * UNROLL + u)
            for k in range(3):
                acc[i, pl.ds(8 * k, 8)] = acc[i, pl.ds(8 * k, 8)] + f[k]
        return 0
    lax.fori_loop(0, (live + UNROLL - 1) // UNROLL, group, 0)

    def finish(t, _):
        rows = pm_ref[t]
        scale = (-0.02 / ROOT) * rows[7:8]
        for k in range(3):
            v = [jnp.sum(acc[2 * t + h, pl.ds(8 * k, 8)], axis=0, keepdims=True) for h in range(2)]
            v = [x + pltpu.roll(x, 64, 1) for x in v]
            f = jnp.where(left[0:1], v[0], v[1]) * scale
            at = pl.ds(k * chunks + t, 1)
            pos_ref[at, :] = rows[3 + k:4 + k]
            frc_ref[at, :] = f
            mom_ref[at, :] = rows[k:k + 1] + 0.25 * f
        return 0
    lax.fori_loop(0, chunks, finish, 0, unroll=8)


def force_call(pairs, count, hlo, hup, pm, lo, up):
    chunks = pm.shape[0]
    smem = pl.BlockSpec(memory_space=pltpu.SMEM)
    vmem = pl.BlockSpec(memory_space=pltpu.VMEM)
    hbm = pl.BlockSpec(memory_space=pl.ANY)
    o = jax.ShapeDtypeStruct((3 * chunks, LANES), jnp.float32)
    return pl.pallas_call(
        force_kernel,
        out_shape=(o, o, o),
        in_specs=[smem] * 4 + [hbm] * 3,
        out_specs=(vmem,) * 3,
        scratch_shapes=[
            pltpu.VMEM((2 * chunks + 2 * HALO + 1, 5, 32, LANES), jnp.float32),
            pltpu.VMEM((2 * chunks, 4, 8, LANES), jnp.float32),
            pltpu.VMEM((2 * chunks, 24, LANES), jnp.float32),
            pltpu.VMEM((chunks, 8, LANES), jnp.float32),
            pltpu.VMEM((2 * HALO, 8, LANES), jnp.float32),
            pltpu.SemaphoreType.DMA((1 + 2 * HALO,)),
        ],
        compiler_params=pltpu.CompilerParams(vmem_limit_bytes=60 * 2**20),
        name="pair_forces",
    )(pairs, count, hlo, hup, pm, lo, up)


def shards(positions, momenta, forces, noise, species, block_pairs, pair_count, halo_blocks):
    flat = [a.reshape(-1, LANES) for a in (positions, momenta, forces, noise)]
    pm, lo, up, hlo, hup = exchange(*flat, species.reshape(-1, LANES), halo_blocks)
    outs = force_call(block_pairs, pair_count, hlo, hup, pm, lo, up)
    return tuple(o.reshape(positions.shape) for o in outs)


def solution(mesh):
    big = P("bead", None, "space")
    in_specs = (big, big, big, big, P("space"), P(None, "space"), P("space"), P(None, "space"))
    return jax.shard_map(shards, mesh=mesh, in_specs=in_specs, out_specs=(big, big, big), check_vma=False)
```

```python
import functools
import math

import jax
import jax.numpy as jnp
import numpy as np
from jax import lax
from jax.experimental import pallas as pl
from jax.experimental.pallas import tpu as pltpu
from jax.sharding import PartitionSpec as P

BLOCK = 64
LANES = 128
HALO = 4
UNROLL = 64
ROOT = math.sqrt(math.log2(math.e))
STEP = 0.5
GAMMA = 0.5
mass_values = (1.0, 0.3, 2.5, 0.75)
strength_values = (1.0, 0.5, 1.5, 0.8)
reach_values = (1.0, 0.6, 1.4, 0.9)
MESH = pl.DeviceIdType.MESH
highest = lax.Precision.HIGHEST


def lookup(values, species):
    out = jnp.full(species.shape, values[3], jnp.float32)
    for k in range(3):
        out = jnp.where(species == k, values[k], out)
    return out


def modes_matrix(n):
    j = np.arange(n)[:, None]
    k = np.arange(n)[None, :]
    phase = 2 * np.pi * (j * k % n) / n
    m = np.where(k < n // 2, np.cos(phase), np.sin(phase)) * math.sqrt(2.0 / n)
    m = np.where(k == 0, math.sqrt(1.0 / n), m)
    m = np.where(k == n // 2, np.where(j % 2 == 0, 1, -1) * math.sqrt(1.0 / n), m)
    return m.astype(np.float32)


def mode_factors(n):
    k = np.arange(n)
    omega = 2 * np.sin(np.pi * k / n)
    gamma = np.where(k == 0, GAMMA, 2 * omega)
    c1 = np.exp(-gamma * STEP)
    c2 = np.sqrt(1 - c1 * c1)
    safe = np.where(k == 0, 1.0, omega)
    drift = np.where(k == 0, STEP, np.sin(omega * STEP) / safe)
    pull = omega * np.sin(omega * STEP)
    turn = np.cos(omega * STEP)
    out = np.zeros((n, LANES), np.float32)
    for c, v in enumerate((c1, c2, turn, drift, pull)):
        out[:, c] = v
    return out


def parts(rows):
    high = rows.astype(jnp.bfloat16).astype(jnp.float32)
    rest = rows - high
    mid = rest.astype(jnp.bfloat16).astype(jnp.float32)
    return high, mid, rest - mid


def pickers():
    row = lax.broadcasted_iota(jnp.int32, (32, LANES), 0)
    lane = lax.broadcasted_iota(jnp.int32, (32, LANES), 1)
    picks = [(lane == 64 * h + row) | (lane == 64 * h + 32 + row) for h in range(2)]
    k = lax.broadcasted_iota(jnp.int32, (2 * LANES, LANES), 0)
    n = lax.broadcasted_iota(jnp.int32, (2 * LANES, LANES), 1)
    return picks, ((k % 64 < 32) == (n < 64)).astype(jnp.bfloat16)


def spread(rows, hs, picks, halves):
    lhs = [
        jnp.concatenate([jnp.where(picks[h], p[c:c + 1], 0.0) for h in hs for c in range(rows.shape[0])],
                        axis=0).astype(jnp.bfloat16)
        for p in parts(rows)
    ]
    out = jnp.dot(jnp.concatenate(lhs[0:2], axis=1), halves, preferred_element_type=jnp.float32)
    return out + jnp.dot(lhs[2], halves[0:LANES], preferred_element_type=jnp.float32)


def exchange_kernel(pos_hbm, mom_hbm, frc_hbm, noise_hbm, sp_hbm, halo_hbm, fixed_hbm,
                    pm_hbm, lo_hbm, up_hbm, hlo_hbm, hup_hbm, tab_hbm,
                    raw, tab, sp_ref, fixed, out_buf, in_buf, back_buf, range_buf, load, store, send1, recv1, send2, recv2, nsend, nrecv):
    beads = lax.axis_size("bead")
    me = lax.axis_index("bead")
    shard = lax.axis_index("space")
    shards = lax.axis_size("space")
    has_lower = shard > 0
    has_upper = shard < shards - 1

    barrier = pltpu.get_barrier_semaphore()

    def each(body, first=1, unroll=4):
        def run(d, _):
            body(d)
            return 0
        lax.fori_loop(first, beads, run, 0, unroll=unroll)

    each(lambda d: pl.semaphore_signal(
        barrier, inc=1, device_id={"bead": lax.rem(me + d, beads)}, device_id_type=MESH))

    for there, other in ((has_lower, shard - 1), (has_upper, shard + 1)):
        @pl.when(there)
        def _(other=other):
            each(lambda d: pl.semaphore_signal(
                barrier, inc=1, device_id={"bead": lax.rem(me + d, beads), "space": other}, device_id_type=MESH), 0)

    loads = [pltpu.make_async_copy(src, dst, load.at[n]) for n, (src, dst) in enumerate((
        (pos_hbm, raw.at[0]), (mom_hbm, raw.at[1]), (frc_hbm, raw.at[2]), (noise_hbm, raw.at[3]),
        (sp_hbm, sp_ref), (fixed_hbm, fixed)))]
    for c in loads:
        c.start()
    for c in loads:
        c.wait()
    for c in range(3):
        s = slice(beads * c, beads * (c + 1))
        out_buf[pl.ds(c, beads, stride=9), :] = raw[0, s]
        out_buf[pl.ds(3 + c, beads, stride=9), :] = raw[1, s] + (0.5 * STEP) * raw[2, s]
        out_buf[pl.ds(6 + c, beads, stride=9), :] = raw[3, s]
    kinds = sp_ref[...]
    range_buf[:, 0, :] = lookup(reach_values, kinds)
    range_buf[:, 1, :] = lookup(strength_values, kinds)
    keep = pltpu.make_async_copy(range_buf, pm_hbm.at[:, 6:8], store.at[0])
    keep.start()

    pl.semaphore_wait(barrier, beads - 1 + beads * (has_lower.astype(jnp.int32) + has_upper.astype(jnp.int32)))

    def first(d):
        j = lax.rem(me + d, beads)
        return pltpu.make_async_remote_copy(
            src_ref=out_buf.at[pl.ds(9 * j, 9)], dst_ref=in_buf.at[pl.ds(9 * me, 9)], send_sem=send1, recv_sem=recv1,
            device_id={"bead": j}, device_id_type=MESH)

    def second(d):
        j = lax.rem(me + d, beads)
        return pltpu.make_async_remote_copy(
            src_ref=back_buf.at[j, 0:6], dst_ref=pm_hbm.at[me, 0:6], send_sem=send2, recv_sem=recv2,
            device_id={"bead": j}, device_id_type=MESH)

    def all_of(buf, rows, sem):
        part = buf.at[0:beads - 1, 0:rows]
        pltpu.make_async_copy(part, part, sem).wait()

    def all_rows(buf, rows, sem):
        part = buf.at[0:rows * (beads - 1)]
        pltpu.make_async_copy(part, part, sem).wait()

    def lists(up):
        return pltpu.make_async_remote_copy(
            src_ref=halo_hbm, dst_ref=hlo_hbm if up else hup_hbm, send_sem=nsend.at[int(up)],
            recv_sem=nrecv.at[int(up)], device_id={"space": shard + 1 if up else shard - 1}, device_id_type=MESH)

    def bounds(up):
        return pltpu.make_async_remote_copy(
            src_ref=range_buf, dst_ref=(lo_hbm if up else up_hbm).at[:, 6:8], send_sem=nsend.at[4 + int(up)],
            recv_sem=nrecv.at[4 + int(up)], device_id={"space": shard + 1 if up else shard - 1}, device_id_type=MESH)

    def beyond(up, d):
        j = lax.rem(me + d, beads)
        return pltpu.make_async_remote_copy(
            src_ref=back_buf.at[j, 3:6], dst_ref=(lo_hbm if up else up_hbm).at[me, 3:6],
            send_sem=nsend.at[2 + int(up)], recv_sem=nrecv.at[2 + int(up)],
            device_id={"bead": j, "space": shard + 1 if up else shard - 1}, device_id_type=MESH)

    def beside(act, receiving=False):
        for up, there in ((True, has_upper), (False, has_lower)):
            if receiving:
                there = has_lower if up else has_upper

            @pl.when(there)
            def _(up=up):
                act(up)

    def all_beyond(buf, sem):
        part = buf.at[:, 3:6]
        pltpu.make_async_copy(part, part, sem).wait()

    each(lambda d: first(d).start())
    beside(lambda up: (lists(up).start(), bounds(up).start()))
    in_buf[pl.ds(9 * me, 9), :] = out_buf[pl.ds(9 * me, 9), :]
    picks, halves = pickers()

    def fill(t, _):
        pair = range_buf[t]
        sign = jnp.where(lax.broadcasted_iota(jnp.int32, pair.shape, 0) == 0, -1.0, 1.0)
        out = spread(pair * sign, (0, 1), picks, halves)
        for h in range(2):
            for c in range(2):
                s = 64 * h + 32 * c
                tab[2 * t + h, c] = out[s:s + 32]
        return 0

    lax.fori_loop(0, range_buf.shape[0], fill, 0, unroll=4)
    tables = pltpu.make_async_copy(tab, tab_hbm, store.at[2])
    tables.start()
    all_rows(in_buf, 9, recv1)

    x = jnp.concatenate([in_buf[pl.ds(r, beads, stride=9), :] for r in range(6)], axis=1)
    xi = jnp.concatenate([in_buf[pl.ds(r, beads, stride=9), :] for r in range(6, 9)], axis=1)
    modes = jnp.dot(fixed[beads:2 * beads, 0:beads], x, precision=highest, preferred_element_type=jnp.float32)
    q, p = modes[:, 0:3 * LANES], modes[:, 3 * LANES:]
    mass = lookup(mass_values, sp_ref[pl.ds(me, 1), :])
    mass3 = jnp.concatenate([mass] * 3, axis=1)
    c1, c2, turn, drift, pull = (fixed[2 * beads:3 * beads, c:c + 1] for c in range(5))
    mixed = c1 * p + c2 * (jnp.sqrt(mass3) * xi)
    q_next = turn * q + drift * (mixed / mass3)
    p_next = turn * mixed - pull * (mass3 * q)
    beads_out = jnp.dot(fixed[0:beads, 0:beads], jnp.concatenate([p_next, q_next], axis=1), precision=highest,
                        preferred_element_type=jnp.float32)
    for r in range(6):
        back_buf[:, r, :] = beads_out[:, LANES * r:LANES * (r + 1)]

    each(lambda d: second(d).start())
    beside(lambda up: each(lambda d: beyond(up, d).start(), 0))
    own = pltpu.make_async_copy(back_buf.at[me, 0:6], pm_hbm.at[me, 0:6], store.at[1])
    own.start()
    all_of(pm_hbm, 6, recv2)
    own.wait()

    all_rows(out_buf, 9, send1)
    beside(lambda up: (lists(up).wait_send(), bounds(up).wait_send()))
    beside(lambda up: (lists(up).wait_recv(), bounds(up).wait_recv()), True)
    all_of(back_buf, 6, send2)
    beside(lambda up: all_beyond(back_buf, nsend.at[2 + int(up)]))
    beside(lambda up: all_beyond(lo_hbm if up else up_hbm, nrecv.at[2 + int(up)]), True)
    keep.wait()
    tables.wait()


def exchange(pos, mom, frc, noise, species, halo):
    beads = lax.axis_size("bead")
    chunks = species.shape[0]
    hbm = pl.BlockSpec(memory_space=pl.ANY)
    f32 = jnp.float32
    block = jax.ShapeDtypeStruct((chunks, 8, LANES), f32)
    ids = jax.ShapeDtypeStruct(halo.shape, jnp.int32)
    table = (2 * chunks, 2, 32, LANES)
    dma = pltpu.SemaphoreType.DMA
    fixed = np.zeros((3, beads, LANES), np.float32)
    fixed[0, :, 0:beads] = modes_matrix(beads)
    fixed[1, :, 0:beads] = modes_matrix(beads).T
    fixed[2] = mode_factors(beads)
    return pl.pallas_call(
        exchange_kernel,
        out_shape=(block, block, block, ids, ids, jax.ShapeDtypeStruct(table, f32)),
        in_specs=[hbm] * 7,
        out_specs=(hbm,) * 6,
        scratch_shapes=[
            pltpu.VMEM((4, 3 * chunks, LANES), f32),
            pltpu.VMEM(table, f32),
            pltpu.VMEM((chunks, LANES), jnp.int32),
            pltpu.VMEM((3 * beads, LANES), f32),
            pltpu.VMEM((beads * 9, LANES), f32),
            pltpu.VMEM((beads * 9, LANES), f32),
            pltpu.VMEM((beads, 8, LANES), f32),
            pltpu.VMEM((chunks, 2, LANES), f32),
            dma((6,)), dma((3,)), dma, dma, dma, dma, dma((6,)), dma((6,)),
        ],
        compiler_params=pltpu.CompilerParams(
            collective_id=0, has_side_effects=True, vmem_limit_bytes=60 * 2**20),
        name="exchange",
    )(pos, mom, frc, noise, species, halo, jnp.asarray(fixed.reshape(3 * beads, LANES)))


def force_kernel(pairs_ref, count_ref, hlo_ref, hup_ref, pm_hbm, lo_hbm, up_hbm, tab_hbm, pos_ref, mom_ref, frc_ref,
                 tab_j, tab_r, tab_i, acc, pm_ref, halo, sem):
    chunks = pm_ref.shape[0]
    blocks = 2 * chunks
    left = lax.broadcasted_iota(jnp.int32, (32, LANES), 1) < 64
    left1 = left[0:8]
    get_own = pltpu.make_async_copy(pm_hbm, pm_ref, sem.at[0])
    get_own.start()
    get_range = pltpu.make_async_copy(tab_hbm, tab_r.at[HALO:HALO + blocks], sem.at[1 + 2 * HALO])
    get_range.start()
    sides = []
    shard = lax.axis_index("space")
    for side in range(2):
        there = shard > 0 if side == 0 else shard < lax.axis_size("space") - 1
        for h in range(HALO):
            b = jnp.where(there, (hup_ref if side else hlo_ref)[1 - side, h], 0)
            get = pltpu.make_async_copy((up_hbm if side else lo_hbm).at[b // 2], halo.at[side * HALO + h], sem.at[1 + side * HALO + h])
            get.start()
            sides.append((get, there, b % 2))

    def clear(i, _):
        acc[i] = jnp.zeros((24, LANES), jnp.float32)
        return 0
    lax.fori_loop(0, blocks, clear, 0, unroll=8)
    tab_j[2 * HALO + blocks] = jnp.zeros(tab_j.shape[1:], jnp.float32)
    tab_r[2 * HALO + blocks] = jnp.zeros(tab_r.shape[1:], jnp.float32)

    picks, halves = pickers()
    kind = lax.broadcasted_iota(jnp.int32, (8, LANES), 0)
    factor = jnp.where(kind < 3, 1.0, jnp.where(kind < 6, ROOT, jnp.where(kind == 6, -1.0, 1.0)))

    get_own.wait()

    def own(t, _):
        m8 = pm_ref[t] * factor
        out = spread(m8[3:6], (0, 1), picks, halves)
        for h in range(2):
            for c in range(3):
                s = 96 * h + 32 * c
                tab_j[HALO + 2 * t + h, c] = out[s:s + 32]
        turned = pltpu.roll(m8, 64, 1)
        for h in range(2):
            both = jnp.where(left1, m8, turned) if h == 0 else jnp.where(left1, turned, m8)
            for c in range(4):
                tab_i[2 * t + h, c] = jnp.broadcast_to(both[3 + c:4 + c], (8, LANES))
        return 0
    lax.fori_loop(0, chunks, own, 0, unroll=16)

    for get, _, _ in sides:
        get.wait()
    for n_, (get, there, half) in enumerate(sides):
        e = n_ if n_ < HALO else blocks + n_
        m8 = jnp.where(there, halo[n_], 0.0) * factor
        m8 = jnp.where(half == 1, pltpu.roll(m8, 64, 1), m8)
        out = spread(m8[3:8], (0,), picks, halves)
        for c in range(5):
            (tab_j if c < 3 else tab_r)[e, c % 3] = out[32 * c:32 * c + 32]
    get_range.wait()

    live = count_ref[0]

    def pair(p):
        i = pairs_ref[0, p]
        j = jnp.where(p < live, pairs_ref[1, p], 2 * HALO + blocks)
        xi, yi, zi, ri = (tab_i[i, c] for c in range(4))
        f = [None] * 3
        for g in range(4):
            s = pl.ds(8 * g, 8)
            dx = xi - tab_j[j, 0, s]
            dy = yi - tab_j[j, 1, s]
            dz = zi - tab_j[j, 2, s]
            d = dx * dx + dy * dy + dz * dz
            inv = 1.0 / (ri + tab_r[j, 0, s])
            w = jnp.exp2(d * inv) * (inv * tab_r[j, 1, s])
            for k, v in enumerate((dx, dy, dz)):
                f[k] = w * v if g == 0 else f[k] + w * v
        return i, f

    def group(g, _):
        for u in range(UNROLL):
            i, f = pair(g * UNROLL + u)
            for k in range(3):
                acc[i, pl.ds(8 * k, 8)] = acc[i, pl.ds(8 * k, 8)] + f[k]
        return 0
    lax.fori_loop(0, (live + UNROLL - 1) // UNROLL, group, 0)

    def finish(t, _):
        rows = pm_ref[t]
        scale = (-0.02 / ROOT) * rows[7:8]
        for k in range(3):
            v = [jnp.sum(acc[2 * t + h, pl.ds(8 * k, 8)], axis=0, keepdims=True) for h in range(2)]
            v = [x + pltpu.roll(x, 64, 1) for x in v]
            f = jnp.where(left[0:1], v[0], v[1]) * scale
            at = pl.ds(k * chunks + t, 1)
            pos_ref[at, :] = rows[3 + k:4 + k]
            frc_ref[at, :] = f
            mom_ref[at, :] = rows[k:k + 1] + 0.25 * f
        return 0
    lax.fori_loop(0, chunks, finish, 0, unroll=8)


def force_call(pairs, count, hlo, hup, pm, lo, up, tab):
    chunks = pm.shape[0]
    smem = pl.BlockSpec(memory_space=pltpu.SMEM)
    vmem = pl.BlockSpec(memory_space=pltpu.VMEM)
    hbm = pl.BlockSpec(memory_space=pl.ANY)
    o = jax.ShapeDtypeStruct((3 * chunks, LANES), jnp.float32)
    return pl.pallas_call(
        force_kernel,
        out_shape=(o, o, o),
        in_specs=[smem] * 4 + [hbm] * 4,
        out_specs=(vmem,) * 3,
        scratch_shapes=[
            pltpu.VMEM((2 * chunks + 2 * HALO + 1, 3, 32, LANES), jnp.float32),
            pltpu.VMEM((2 * chunks + 2 * HALO + 1, 2, 32, LANES), jnp.float32),
            pltpu.VMEM((2 * chunks, 4, 8, LANES), jnp.float32),
            pltpu.VMEM((2 * chunks, 24, LANES), jnp.float32),
            pltpu.VMEM((chunks, 8, LANES), jnp.float32),
            pltpu.VMEM((2 * HALO, 8, LANES), jnp.float32),
            pltpu.SemaphoreType.DMA((2 + 2 * HALO,)),
        ],
        compiler_params=pltpu.CompilerParams(vmem_limit_bytes=60 * 2**20),
        name="pair_forces",
    )(pairs, count, hlo, hup, pm, lo, up, tab)


def shards(positions, momenta, forces, noise, species, block_pairs, pair_count, halo_blocks):
    flat = [a.reshape(-1, LANES) for a in (positions, momenta, forces, noise)]
    pm, lo, up, hlo, hup, tab = exchange(*flat, species.reshape(-1, LANES), halo_blocks)
    outs = force_call(block_pairs, pair_count, hlo, hup, pm, lo, up, tab)
    return tuple(o.reshape(positions.shape) for o in outs)


def solution(mesh):
    big = P("bead", None, "space")
    in_specs = (big, big, big, big, P("space"), P(None, "space"), P("space"), P(None, "space"))
    return jax.shard_map(shards, mesh=mesh, in_specs=in_specs, out_specs=(big, big, big), check_vma=False)
```

```python
import functools
import math

import jax
import jax.numpy as jnp
import numpy as np
from jax import lax
from jax.experimental import pallas as pl
from jax.experimental.pallas import tpu as pltpu
from jax.sharding import PartitionSpec as P

BLOCK = 64
LANES = 128
HALO = 4
UNROLL = 64
ROOT = math.sqrt(math.log2(math.e))
STEP = 0.5
GAMMA = 0.5
mass_values = (1.0, 0.3, 2.5, 0.75)
strength_values = (1.0, 0.5, 1.5, 0.8)
reach_values = (1.0, 0.6, 1.4, 0.9)
MESH = pl.DeviceIdType.MESH
highest = lax.Precision.HIGHEST


def lookup(values, species):
    out = jnp.full(species.shape, values[3], jnp.float32)
    for k in range(3):
        out = jnp.where(species == k, values[k], out)
    return out


def modes_matrix(n):
    j = np.arange(n)[:, None]
    k = np.arange(n)[None, :]
    phase = 2 * np.pi * (j * k % n) / n
    m = np.where(k < n // 2, np.cos(phase), np.sin(phase)) * math.sqrt(2.0 / n)
    m = np.where(k == 0, math.sqrt(1.0 / n), m)
    m = np.where(k == n // 2, np.where(j % 2 == 0, 1, -1) * math.sqrt(1.0 / n), m)
    return m.astype(np.float32)


def mode_factors(n):
    k = np.arange(n)
    omega = 2 * np.sin(np.pi * k / n)
    gamma = np.where(k == 0, GAMMA, 2 * omega)
    c1 = np.exp(-gamma * STEP)
    c2 = np.sqrt(1 - c1 * c1)
    safe = np.where(k == 0, 1.0, omega)
    drift = np.where(k == 0, STEP, np.sin(omega * STEP) / safe)
    pull = omega * np.sin(omega * STEP)
    turn = np.cos(omega * STEP)
    out = np.zeros((n, LANES), np.float32)
    for c, v in enumerate((c1, c2, turn, drift, pull)):
        out[:, c] = v
    return out


def parts(rows):
    high = rows.astype(jnp.bfloat16).astype(jnp.float32)
    rest = rows - high
    mid = rest.astype(jnp.bfloat16).astype(jnp.float32)
    return high, mid, rest - mid


def pickers():
    row = lax.broadcasted_iota(jnp.int32, (32, LANES), 0)
    lane = lax.broadcasted_iota(jnp.int32, (32, LANES), 1)
    picks = [(lane == 64 * h + row) | (lane == 64 * h + 32 + row) for h in range(2)]
    k = lax.broadcasted_iota(jnp.int32, (2 * LANES, LANES), 0)
    n = lax.broadcasted_iota(jnp.int32, (2 * LANES, LANES), 1)
    return picks, ((k % 64 < 32) == (n < 64)).astype(jnp.bfloat16)


def spread(rows, hs, picks, halves):
    lhs = [
        jnp.concatenate([jnp.where(picks[h], p[c:c + 1], 0.0) for h in hs for c in range(rows.shape[0])],
                        axis=0).astype(jnp.bfloat16)
        for p in parts(rows)
    ]
    out = jnp.dot(jnp.concatenate(lhs[0:2], axis=1), halves, preferred_element_type=jnp.float32)
    return out + jnp.dot(lhs[2], halves[0:LANES], preferred_element_type=jnp.float32)


def exchange_kernel(pos_hbm, mom_hbm, frc_hbm, noise_hbm, sp_hbm, halo_hbm, fixed_hbm,
                    pm_hbm, lo_hbm, up_hbm, hlo_hbm, hup_hbm, tab_hbm,
                    raw, tab, sp_ref, fixed, out_buf, in_buf, back_buf, range_buf, load, store, send1, recv1, send2, recv2, nsend, nrecv, ready):
    beads = lax.axis_size("bead")
    me = lax.axis_index("bead")
    shard = lax.axis_index("space")
    shards = lax.axis_size("space")
    has_lower = shard > 0
    has_upper = shard < shards - 1

    loads = [pltpu.make_async_copy(src, dst, load.at[n]) for n, (src, dst) in enumerate((
        (pos_hbm, raw.at[0]), (mom_hbm, raw.at[1]), (frc_hbm, raw.at[2]), (noise_hbm, raw.at[3]),
        (sp_hbm, sp_ref), (fixed_hbm, fixed)))]
    for c in loads:
        c.start()

    barrier = pltpu.get_barrier_semaphore()

    def each(body, first=1, unroll=4):
        def run(d, _):
            body(d)
            return 0
        lax.fori_loop(first, beads, run, 0, unroll=unroll)

    each(lambda d: pl.semaphore_signal(
        barrier, inc=1, device_id={"bead": lax.rem(me + d, beads)}, device_id_type=MESH))

    for there, other in ((has_lower, shard - 1), (has_upper, shard + 1)):
        @pl.when(there)
        def _(other=other):
            pl.semaphore_signal(barrier, inc=1, device_id={"space": other}, device_id_type=MESH)

    for c in loads:
        c.wait()
    for c in range(3):
        s = slice(beads * c, beads * (c + 1))
        out_buf[pl.ds(c, beads, stride=9), :] = raw[0, s]
        out_buf[pl.ds(3 + c, beads, stride=9), :] = raw[1, s] + (0.5 * STEP) * raw[2, s]
        out_buf[pl.ds(6 + c, beads, stride=9), :] = raw[3, s]
    beside_count = has_lower.astype(jnp.int32) + has_upper.astype(jnp.int32)
    pl.semaphore_wait(barrier, beads - 1 + beside_count)
    for there, other in ((has_lower, shard - 1), (has_upper, shard + 1)):
        @pl.when(there)
        def _(other=other):
            pl.semaphore_signal(ready, inc=1, device_id={"space": other}, device_id_type=MESH)


    def first(d):
        j = lax.rem(me + d, beads)
        return pltpu.make_async_remote_copy(
            src_ref=out_buf.at[pl.ds(9 * j, 9)], dst_ref=in_buf.at[pl.ds(9 * me, 9)], send_sem=send1, recv_sem=recv1,
            device_id={"bead": j}, device_id_type=MESH)

    def second(d):
        j = lax.rem(me + d, beads)
        return pltpu.make_async_remote_copy(
            src_ref=back_buf.at[j, 0:6], dst_ref=pm_hbm.at[me, 0:6], send_sem=send2, recv_sem=recv2,
            device_id={"bead": j}, device_id_type=MESH)

    def all_of(buf, rows, sem):
        part = buf.at[0:beads - 1, 0:rows]
        pltpu.make_async_copy(part, part, sem).wait()

    def all_rows(buf, rows, sem):
        part = buf.at[0:rows * (beads - 1)]
        pltpu.make_async_copy(part, part, sem).wait()

    def lists(up):
        return pltpu.make_async_remote_copy(
            src_ref=halo_hbm, dst_ref=hlo_hbm if up else hup_hbm, send_sem=nsend.at[int(up)],
            recv_sem=nrecv.at[int(up)], device_id={"space": shard + 1 if up else shard - 1}, device_id_type=MESH)

    def bounds(up):
        return pltpu.make_async_remote_copy(
            src_ref=range_buf, dst_ref=(lo_hbm if up else up_hbm).at[:, 6:8], send_sem=nsend.at[4 + int(up)],
            recv_sem=nrecv.at[4 + int(up)], device_id={"space": shard + 1 if up else shard - 1}, device_id_type=MESH)

    def beyond(up, d):
        j = lax.rem(me + d, beads)
        return pltpu.make_async_remote_copy(
            src_ref=back_buf.at[j, 3:6], dst_ref=(lo_hbm if up else up_hbm).at[me, 3:6],
            send_sem=nsend.at[2 + int(up)], recv_sem=nrecv.at[2 + int(up)],
            device_id={"bead": j, "space": shard + 1 if up else shard - 1}, device_id_type=MESH)

    def beside(act, receiving=False):
        for up, there in ((True, has_upper), (False, has_lower)):
            if receiving:
                there = has_lower if up else has_upper

            @pl.when(there)
            def _(up=up):
                act(up)

    def all_beyond(buf, sem):
        part = buf.at[:, 3:6]
        pltpu.make_async_copy(part, part, sem).wait()

    each(lambda d: first(d).start())
    kinds = sp_ref[...]
    range_buf[:, 0, :] = lookup(reach_values, kinds)
    range_buf[:, 1, :] = lookup(strength_values, kinds)
    keep = pltpu.make_async_copy(range_buf, pm_hbm.at[:, 6:8], store.at[0])
    keep.start()
    beside(lambda up: (lists(up).start(), bounds(up).start()))
    in_buf[pl.ds(9 * me, 9), :] = out_buf[pl.ds(9 * me, 9), :]
    picks, halves = pickers()

    def fill(t, _):
        pair = range_buf[t]
        sign = jnp.where(lax.broadcasted_iota(jnp.int32, pair.shape, 0) == 0, -1.0, 1.0)
        out = spread(pair * sign, (0, 1), picks, halves)
        for h in range(2):
            for c in range(2):
                s = 64 * h + 32 * c
                tab[2 * t + h, c] = out[s:s + 32]
        return 0

    lax.fori_loop(0, range_buf.shape[0], fill, 0, unroll=4)
    tables = pltpu.make_async_copy(tab, tab_hbm, store.at[2])
    tables.start()
    all_rows(in_buf, 9, recv1)

    x = jnp.concatenate([in_buf[pl.ds(r, beads, stride=9), :] for r in range(6)], axis=1)
    xi = jnp.concatenate([in_buf[pl.ds(r, beads, stride=9), :] for r in range(6, 9)], axis=1)
    modes = jnp.dot(fixed[beads:2 * beads, 0:beads], x, precision=highest, preferred_element_type=jnp.float32)
    q, p = modes[:, 0:3 * LANES], modes[:, 3 * LANES:]
    mass = lookup(mass_values, sp_ref[pl.ds(me, 1), :])
    mass3 = jnp.concatenate([mass] * 3, axis=1)
    c1, c2, turn, drift, pull = (fixed[2 * beads:3 * beads, c:c + 1] for c in range(5))
    mixed = c1 * p + c2 * (jnp.sqrt(mass3) * xi)
    q_next = turn * q + drift * (mixed / mass3)
    p_next = turn * mixed - pull * (mass3 * q)
    beads_out = jnp.dot(fixed[0:beads, 0:beads], jnp.concatenate([p_next, q_next], axis=1), precision=highest,
                        preferred_element_type=jnp.float32)
    for r in range(6):
        back_buf[:, r, :] = beads_out[:, LANES * r:LANES * (r + 1)]

    each(lambda d: second(d).start())
    pl.semaphore_wait(ready, beside_count)
    beside(lambda up: each(lambda d: beyond(up, d).start(), 0))
    own = pltpu.make_async_copy(back_buf.at[me, 0:6], pm_hbm.at[me, 0:6], store.at[1])
    own.start()
    all_of(pm_hbm, 6, recv2)
    own.wait()

    all_rows(out_buf, 9, send1)
    beside(lambda up: (lists(up).wait_send(), bounds(up).wait_send()))
    beside(lambda up: (lists(up).wait_recv(), bounds(up).wait_recv()), True)
    all_of(back_buf, 6, send2)
    beside(lambda up: all_beyond(back_buf, nsend.at[2 + int(up)]))
    beside(lambda up: all_beyond(lo_hbm if up else up_hbm, nrecv.at[2 + int(up)]), True)
    keep.wait()
    tables.wait()


def exchange(pos, mom, frc, noise, species, halo):
    beads = lax.axis_size("bead")
    chunks = species.shape[0]
    hbm = pl.BlockSpec(memory_space=pl.ANY)
    f32 = jnp.float32
    block = jax.ShapeDtypeStruct((chunks, 8, LANES), f32)
    ids = jax.ShapeDtypeStruct(halo.shape, jnp.int32)
    table = (2 * chunks, 2, 32, LANES)
    dma = pltpu.SemaphoreType.DMA
    fixed = np.zeros((3, beads, LANES), np.float32)
    fixed[0, :, 0:beads] = modes_matrix(beads)
    fixed[1, :, 0:beads] = modes_matrix(beads).T
    fixed[2] = mode_factors(beads)
    return pl.pallas_call(
        exchange_kernel,
        out_shape=(block, block, block, ids, ids, jax.ShapeDtypeStruct(table, f32)),
        in_specs=[hbm] * 7,
        out_specs=(hbm,) * 6,
        scratch_shapes=[
            pltpu.VMEM((4, 3 * chunks, LANES), f32),
            pltpu.VMEM(table, f32),
            pltpu.VMEM((chunks, LANES), jnp.int32),
            pltpu.VMEM((3 * beads, LANES), f32),
            pltpu.VMEM((beads * 9, LANES), f32),
            pltpu.VMEM((beads * 9, LANES), f32),
            pltpu.VMEM((beads, 8, LANES), f32),
            pltpu.VMEM((chunks, 2, LANES), f32),
            dma((6,)), dma((3,)), dma, dma, dma, dma, dma((6,)), dma((6,)), pltpu.SemaphoreType.REGULAR,
        ],
        compiler_params=pltpu.CompilerParams(
            collective_id=0, has_side_effects=True, vmem_limit_bytes=60 * 2**20),
        name="exchange",
    )(pos, mom, frc, noise, species, halo, jnp.asarray(fixed.reshape(3 * beads, LANES)))


def force_kernel(pairs_ref, count_ref, hlo_ref, hup_ref, pm_hbm, lo_hbm, up_hbm, tab_hbm, pos_ref, mom_ref, frc_ref,
                 tab_j, tab_r, tab_i, acc, pm_ref, halo, sem):
    chunks = pm_ref.shape[0]
    blocks = 2 * chunks
    left = lax.broadcasted_iota(jnp.int32, (32, LANES), 1) < 64
    left1 = left[0:8]
    get_own = pltpu.make_async_copy(pm_hbm, pm_ref, sem.at[0])
    get_own.start()
    get_range = pltpu.make_async_copy(tab_hbm, tab_r.at[HALO:HALO + blocks], sem.at[1 + 2 * HALO])
    get_range.start()
    sides = []
    shard = lax.axis_index("space")
    for side in range(2):
        there = shard > 0 if side == 0 else shard < lax.axis_size("space") - 1
        for h in range(HALO):
            b = jnp.where(there, (hup_ref if side else hlo_ref)[1 - side, h], 0)
            get = pltpu.make_async_copy((up_hbm if side else lo_hbm).at[b // 2], halo.at[side * HALO + h], sem.at[1 + side * HALO + h])
            get.start()
            sides.append((get, there, b % 2))

    def clear(i, _):
        acc[i] = jnp.zeros((24, LANES), jnp.float32)
        return 0
    lax.fori_loop(0, blocks, clear, 0, unroll=8)
    tab_j[2 * HALO + blocks] = jnp.zeros(tab_j.shape[1:], jnp.float32)
    tab_r[2 * HALO + blocks] = jnp.zeros(tab_r.shape[1:], jnp.float32)

    picks, halves = pickers()
    kind = lax.broadcasted_iota(jnp.int32, (8, LANES), 0)
    factor = jnp.where(kind < 3, 1.0, jnp.where(kind < 6, ROOT, jnp.where(kind == 6, -1.0, 1.0)))

    get_own.wait()

    def own(t, _):
        m8 = pm_ref[t] * factor
        out = spread(m8[3:6], (0, 1), picks, halves)
        for h in range(2):
            for c in range(3):
                s = 96 * h + 32 * c
                tab_j[HALO + 2 * t + h, c] = out[s:s + 32]
        turned = pltpu.roll(m8, 64, 1)
        for h in range(2):
            both = jnp.where(left1, m8, turned) if h == 0 else jnp.where(left1, turned, m8)
            for c in range(4):
                tab_i[2 * t + h, c] = jnp.broadcast_to(both[3 + c:4 + c], (8, LANES))
        return 0
    lax.fori_loop(0, chunks, own, 0, unroll=16)

    for get, _, _ in sides:
        get.wait()
    for n_, (get, there, half) in enumerate(sides):
        e = n_ if n_ < HALO else blocks + n_
        m8 = jnp.where(there, halo[n_], 0.0) * factor
        m8 = jnp.where(half == 1, pltpu.roll(m8, 64, 1), m8)
        out = spread(m8[3:8], (0,), picks, halves)
        for c in range(5):
            (tab_j if c < 3 else tab_r)[e, c % 3] = out[32 * c:32 * c + 32]
    get_range.wait()

    live = count_ref[0]

    def pair(p):
        i = pairs_ref[0, p]
        j = jnp.where(p < live, pairs_ref[1, p], 2 * HALO + blocks)
        xi, yi, zi, ri = (tab_i[i, c] for c in range(4))
        f = [None] * 3
        for g in range(4):
            s = pl.ds(8 * g, 8)
            dx = xi - tab_j[j, 0, s]
            dy = yi - tab_j[j, 1, s]
            dz = zi - tab_j[j, 2, s]
            d = dx * dx + dy * dy + dz * dz
            inv = 1.0 / (ri + tab_r[j, 0, s])
            w = jnp.exp2(d * inv) * (inv * tab_r[j, 1, s])
            for k, v in enumerate((dx, dy, dz)):
                f[k] = w * v if g == 0 else f[k] + w * v
        return i, f

    def group(g, _):
        for u in range(UNROLL):
            i, f = pair(g * UNROLL + u)
            for k in range(3):
                acc[i, pl.ds(8 * k, 8)] = acc[i, pl.ds(8 * k, 8)] + f[k]
        return 0
    lax.fori_loop(0, (live + UNROLL - 1) // UNROLL, group, 0)

    def finish(t, _):
        rows = pm_ref[t]
        scale = (-0.02 / ROOT) * rows[7:8]
        for k in range(3):
            v = [jnp.sum(acc[2 * t + h, pl.ds(8 * k, 8)], axis=0, keepdims=True) for h in range(2)]
            v = [x + pltpu.roll(x, 64, 1) for x in v]
            f = jnp.where(left[0:1], v[0], v[1]) * scale
            at = pl.ds(k * chunks + t, 1)
            pos_ref[at, :] = rows[3 + k:4 + k]
            frc_ref[at, :] = f
            mom_ref[at, :] = rows[k:k + 1] + 0.25 * f
        return 0
    lax.fori_loop(0, chunks, finish, 0, unroll=8)


def force_call(pairs, count, hlo, hup, pm, lo, up, tab):
    chunks = pm.shape[0]
    smem = pl.BlockSpec(memory_space=pltpu.SMEM)
    vmem = pl.BlockSpec(memory_space=pltpu.VMEM)
    hbm = pl.BlockSpec(memory_space=pl.ANY)
    o = jax.ShapeDtypeStruct((3 * chunks, LANES), jnp.float32)
    return pl.pallas_call(
        force_kernel,
        out_shape=(o, o, o),
        in_specs=[smem] * 4 + [hbm] * 4,
        out_specs=(vmem,) * 3,
        scratch_shapes=[
            pltpu.VMEM((2 * chunks + 2 * HALO + 1, 3, 32, LANES), jnp.float32),
            pltpu.VMEM((2 * chunks + 2 * HALO + 1, 2, 32, LANES), jnp.float32),
            pltpu.VMEM((2 * chunks, 4, 8, LANES), jnp.float32),
            pltpu.VMEM((2 * chunks, 24, LANES), jnp.float32),
            pltpu.VMEM((chunks, 8, LANES), jnp.float32),
            pltpu.VMEM((2 * HALO, 8, LANES), jnp.float32),
            pltpu.SemaphoreType.DMA((2 + 2 * HALO,)),
        ],
        compiler_params=pltpu.CompilerParams(vmem_limit_bytes=60 * 2**20),
        name="pair_forces",
    )(pairs, count, hlo, hup, pm, lo, up, tab)


def shards(positions, momenta, forces, noise, species, block_pairs, pair_count, halo_blocks):
    flat = [a.reshape(-1, LANES) for a in (positions, momenta, forces, noise)]
    pm, lo, up, hlo, hup, tab = exchange(*flat, species.reshape(-1, LANES), halo_blocks)
    outs = force_call(block_pairs, pair_count, hlo, hup, pm, lo, up, tab)
    return tuple(o.reshape(positions.shape) for o in outs)


def solution(mesh):
    big = P("bead", None, "space")
    in_specs = (big, big, big, big, P("space"), P(None, "space"), P("space"), P(None, "space"))
    return jax.shard_map(shards, mesh=mesh, in_specs=in_specs, out_specs=(big, big, big), check_vma=False)
```

```python
import functools
import math

import jax
import jax.numpy as jnp
import numpy as np
from jax import lax
from jax.experimental import pallas as pl
from jax.experimental.pallas import tpu as pltpu
from jax.sharding import PartitionSpec as P

BLOCK = 64
LANES = 128
HALO = 4
UNROLL = 64
ROOT = math.sqrt(math.log2(math.e))
STEP = 0.5
GAMMA = 0.5
mass_values = (1.0, 0.3, 2.5, 0.75)
strength_values = (1.0, 0.5, 1.5, 0.8)
reach_values = (1.0, 0.6, 1.4, 0.9)
MESH = pl.DeviceIdType.MESH
highest = lax.Precision.HIGHEST


def lookup(values, species):
    out = jnp.full(species.shape, values[3], jnp.float32)
    for k in range(3):
        out = jnp.where(species == k, values[k], out)
    return out


def modes_matrix(n):
    j = np.arange(n)[:, None]
    k = np.arange(n)[None, :]
    phase = 2 * np.pi * (j * k % n) / n
    m = np.where(k < n // 2, np.cos(phase), np.sin(phase)) * math.sqrt(2.0 / n)
    m = np.where(k == 0, math.sqrt(1.0 / n), m)
    m = np.where(k == n // 2, np.where(j % 2 == 0, 1, -1) * math.sqrt(1.0 / n), m)
    return m.astype(np.float32)


def mode_factors(n):
    k = np.arange(n)
    omega = 2 * np.sin(np.pi * k / n)
    gamma = np.where(k == 0, GAMMA, 2 * omega)
    c1 = np.exp(-gamma * STEP)
    c2 = np.sqrt(1 - c1 * c1)
    safe = np.where(k == 0, 1.0, omega)
    drift = np.where(k == 0, STEP, np.sin(omega * STEP) / safe)
    pull = omega * np.sin(omega * STEP)
    turn = np.cos(omega * STEP)
    out = np.zeros((n, LANES), np.float32)
    for c, v in enumerate((c1, c2, turn, drift, pull)):
        out[:, c] = v
    return out


def parts(rows):
    high = rows.astype(jnp.bfloat16).astype(jnp.float32)
    rest = rows - high
    mid = rest.astype(jnp.bfloat16).astype(jnp.float32)
    return high, mid, rest - mid


def pickers():
    row = lax.broadcasted_iota(jnp.int32, (32, LANES), 0)
    lane = lax.broadcasted_iota(jnp.int32, (32, LANES), 1)
    picks = [(lane == 64 * h + row) | (lane == 64 * h + 32 + row) for h in range(2)]
    k = lax.broadcasted_iota(jnp.int32, (2 * LANES, LANES), 0)
    n = lax.broadcasted_iota(jnp.int32, (2 * LANES, LANES), 1)
    return picks, ((k % 64 < 32) == (n < 64)).astype(jnp.bfloat16)


def spread(rows, hs, picks, halves):
    lhs = [
        jnp.concatenate([jnp.where(picks[h], p[c:c + 1], 0.0) for h in hs for c in range(rows.shape[0])],
                        axis=0).astype(jnp.bfloat16)
        for p in parts(rows)
    ]
    out = jnp.dot(jnp.concatenate(lhs[0:2], axis=1), halves, preferred_element_type=jnp.float32)
    return out + jnp.dot(lhs[2], halves[0:LANES], preferred_element_type=jnp.float32)


def exchange_kernel(pos_hbm, mom_hbm, frc_hbm, noise_hbm, sp_hbm, halo_hbm, fixed_hbm,
                    pm_hbm, lo_hbm, up_hbm, hlo_hbm, hup_hbm, tab_hbm,
                    raw, tab, sp_ref, fixed, out_buf, in_buf, back_buf, range_buf, load, store, send1, recv1, send2, recv2, nsend, nrecv, ready):
    beads = lax.axis_size("bead")
    me = lax.axis_index("bead")
    shard = lax.axis_index("space")
    shards = lax.axis_size("space")
    has_lower = shard > 0
    has_upper = shard < shards - 1

    loads = [pltpu.make_async_copy(src, dst, load.at[n]) for n, (src, dst) in enumerate((
        (pos_hbm, raw.at[0]), (mom_hbm, raw.at[1]), (frc_hbm, raw.at[2]), (noise_hbm, raw.at[3]),
        (sp_hbm, sp_ref), (fixed_hbm, fixed)))]
    for c in loads:
        c.start()

    barrier = pltpu.get_barrier_semaphore()

    def each(body, first=1, unroll=4):
        def run(d, _):
            body(d)
            return 0
        lax.fori_loop(first, beads, run, 0, unroll=unroll)

    each(lambda d: pl.semaphore_signal(
        barrier, inc=1, device_id={"bead": lax.rem(me + d, beads)}, device_id_type=MESH))

    for there, other in ((has_lower, shard - 1), (has_upper, shard + 1)):
        @pl.when(there)
        def _(other=other):
            pl.semaphore_signal(barrier, inc=1, device_id={"space": other}, device_id_type=MESH)

    for c in loads:
        c.wait()
    for c in range(3):
        s = slice(beads * c, beads * (c + 1))
        out_buf[pl.ds(c, beads, stride=9), :] = raw[0, s]
        out_buf[pl.ds(3 + c, beads, stride=9), :] = raw[1, s] + (0.5 * STEP) * raw[2, s]
        out_buf[pl.ds(6 + c, beads, stride=9), :] = raw[3, s]
    beside_count = has_lower.astype(jnp.int32) + has_upper.astype(jnp.int32)
    pl.semaphore_wait(barrier, beads - 1 + beside_count)
    for there, other in ((has_lower, shard - 1), (has_upper, shard + 1)):
        @pl.when(there)
        def _(other=other):
            pl.semaphore_signal(ready, inc=1, device_id={"space": other}, device_id_type=MESH)


    def first(d):
        j = lax.rem(me + d, beads)
        return pltpu.make_async_remote_copy(
            src_ref=out_buf.at[pl.ds(9 * j, 9)], dst_ref=in_buf.at[pl.ds(9 * me, 9)], send_sem=send1, recv_sem=recv1,
            device_id={"bead": j}, device_id_type=MESH)

    def second(d):
        j = lax.rem(me + d, beads)
        return pltpu.make_async_remote_copy(
            src_ref=back_buf.at[j, 0:6], dst_ref=pm_hbm.at[me, 0:6], send_sem=send2, recv_sem=recv2,
            device_id={"bead": j}, device_id_type=MESH)

    def all_of(buf, rows, sem):
        part = buf.at[0:beads - 1, 0:rows]
        pltpu.make_async_copy(part, part, sem).wait()

    def all_rows(buf, rows, sem):
        part = buf.at[0:rows * (beads - 1)]
        pltpu.make_async_copy(part, part, sem).wait()

    def lists(up):
        return pltpu.make_async_remote_copy(
            src_ref=halo_hbm, dst_ref=hlo_hbm if up else hup_hbm, send_sem=nsend.at[int(up)],
            recv_sem=nrecv.at[int(up)], device_id={"space": shard + 1 if up else shard - 1}, device_id_type=MESH)

    def bounds(up):
        return pltpu.make_async_remote_copy(
            src_ref=range_buf, dst_ref=(lo_hbm if up else up_hbm).at[:, 6:8], send_sem=nsend.at[4 + int(up)],
            recv_sem=nrecv.at[4 + int(up)], device_id={"space": shard + 1 if up else shard - 1}, device_id_type=MESH)

    def beyond(up, d):
        j = lax.rem(me + d, beads)
        return pltpu.make_async_remote_copy(
            src_ref=back_buf.at[j, 3:6], dst_ref=(lo_hbm if up else up_hbm).at[me, 3:6],
            send_sem=nsend.at[2 + int(up)], recv_sem=nrecv.at[2 + int(up)],
            device_id={"bead": j, "space": shard + 1 if up else shard - 1}, device_id_type=MESH)

    def beside(act, receiving=False):
        for up, there in ((True, has_upper), (False, has_lower)):
            if receiving:
                there = has_lower if up else has_upper

            @pl.when(there)
            def _(up=up):
                act(up)

    def all_beyond(buf, sem):
        part = buf.at[:, 3:6]
        pltpu.make_async_copy(part, part, sem).wait()

    each(lambda d: first(d).start())
    kinds = sp_ref[...]
    range_buf[:, 0, :] = lookup(reach_values, kinds)
    range_buf[:, 1, :] = lookup(strength_values, kinds)
    keep = pltpu.make_async_copy(range_buf, pm_hbm.at[:, 6:8], store.at[0])
    keep.start()
    beside(lambda up: (lists(up).start(), bounds(up).start()))
    in_buf[pl.ds(9 * me, 9), :] = out_buf[pl.ds(9 * me, 9), :]
    picks, halves = pickers()

    def fill(t, _):
        pair = range_buf[t]
        sign = jnp.where(lax.broadcasted_iota(jnp.int32, pair.shape, 0) == 0, -1.0, 1.0)
        out = spread(pair * sign, (0, 1), picks, halves)
        for h in range(2):
            for c in range(2):
                s = 64 * h + 32 * c
                tab[2 * t + h, c] = out[s:s + 32]
        return 0

    lax.fori_loop(0, range_buf.shape[0], fill, 0, unroll=4)
    tables = pltpu.make_async_copy(tab, tab_hbm, store.at[2])
    tables.start()
    all_rows(in_buf, 9, recv1)

    x = jnp.concatenate([in_buf[pl.ds(r, beads, stride=9), :] for r in range(6)], axis=1)
    xi = jnp.concatenate([in_buf[pl.ds(r, beads, stride=9), :] for r in range(6, 9)], axis=1)
    modes = jnp.dot(fixed[beads:2 * beads, 0:beads], x, precision=highest, preferred_element_type=jnp.float32)
    q, p = modes[:, 0:3 * LANES], modes[:, 3 * LANES:]
    mass = lookup(mass_values, sp_ref[pl.ds(me, 1), :])
    mass3 = jnp.concatenate([mass] * 3, axis=1)
    c1, c2, turn, drift, pull = (fixed[2 * beads:3 * beads, c:c + 1] for c in range(5))
    mixed = c1 * p + c2 * (jnp.sqrt(mass3) * xi)
    q_next = turn * q + drift * (mixed / mass3)
    p_next = turn * mixed - pull * (mass3 * q)
    beads_out = jnp.dot(fixed[0:beads, 0:beads], jnp.concatenate([p_next, q_next], axis=1), precision=highest,
                        preferred_element_type=jnp.float32)
    for r in range(6):
        back_buf[:, r, :] = beads_out[:, LANES * r:LANES * (r + 1)]

    pl.semaphore_wait(ready, beside_count)
    beside(lambda up: beyond(up, 0).start())

    def send(d):
        second(d).start()
        beside(lambda up: beyond(up, d).start())

    each(send)
    own = pltpu.make_async_copy(back_buf.at[me, 0:6], pm_hbm.at[me, 0:6], store.at[1])
    own.start()
    all_of(pm_hbm, 6, recv2)
    own.wait()

    all_rows(out_buf, 9, send1)
    beside(lambda up: (lists(up).wait_send(), bounds(up).wait_send()))
    beside(lambda up: (lists(up).wait_recv(), bounds(up).wait_recv()), True)
    all_of(back_buf, 6, send2)
    beside(lambda up: all_beyond(back_buf, nsend.at[2 + int(up)]))
    beside(lambda up: all_beyond(lo_hbm if up else up_hbm, nrecv.at[2 + int(up)]), True)
    keep.wait()
    tables.wait()


def exchange(pos, mom, frc, noise, species, halo):
    beads = lax.axis_size("bead")
    chunks = species.shape[0]
    hbm = pl.BlockSpec(memory_space=pl.ANY)
    f32 = jnp.float32
    block = jax.ShapeDtypeStruct((chunks, 8, LANES), f32)
    ids = jax.ShapeDtypeStruct(halo.shape, jnp.int32)
    table = (2 * chunks, 2, 32, LANES)
    dma = pltpu.SemaphoreType.DMA
    fixed = np.zeros((3, beads, LANES), np.float32)
    fixed[0, :, 0:beads] = modes_matrix(beads)
    fixed[1, :, 0:beads] = modes_matrix(beads).T
    fixed[2] = mode_factors(beads)
    return pl.pallas_call(
        exchange_kernel,
        out_shape=(block, block, block, ids, ids, jax.ShapeDtypeStruct(table, f32)),
        in_specs=[hbm] * 7,
        out_specs=(hbm,) * 6,
        scratch_shapes=[
            pltpu.VMEM((4, 3 * chunks, LANES), f32),
            pltpu.VMEM(table, f32),
            pltpu.VMEM((chunks, LANES), jnp.int32),
            pltpu.VMEM((3 * beads, LANES), f32),
            pltpu.VMEM((beads * 9, LANES), f32),
            pltpu.VMEM((beads * 9, LANES), f32),
            pltpu.VMEM((beads, 8, LANES), f32),
            pltpu.VMEM((chunks, 2, LANES), f32),
            dma((6,)), dma((3,)), dma, dma, dma, dma, dma((6,)), dma((6,)), pltpu.SemaphoreType.REGULAR,
        ],
        compiler_params=pltpu.CompilerParams(
            collective_id=0, has_side_effects=True, vmem_limit_bytes=60 * 2**20),
        name="exchange",
    )(pos, mom, frc, noise, species, halo, jnp.asarray(fixed.reshape(3 * beads, LANES)))


def force_kernel(pairs_ref, count_ref, hlo_ref, hup_ref, pm_hbm, lo_hbm, up_hbm, tab_hbm, pos_ref, mom_ref, frc_ref,
                 tab_j, tab_r, tab_i, acc, pm_ref, halo, sem):
    chunks = pm_ref.shape[0]
    blocks = 2 * chunks
    left = lax.broadcasted_iota(jnp.int32, (32, LANES), 1) < 64
    left1 = left[0:8]
    get_own = pltpu.make_async_copy(pm_hbm, pm_ref, sem.at[0])
    get_own.start()
    get_range = pltpu.make_async_copy(tab_hbm, tab_r.at[HALO:HALO + blocks], sem.at[1 + 2 * HALO])
    get_range.start()
    sides = []
    shard = lax.axis_index("space")
    for side in range(2):
        there = shard > 0 if side == 0 else shard < lax.axis_size("space") - 1
        for h in range(HALO):
            b = jnp.where(there, (hup_ref if side else hlo_ref)[1 - side, h], 0)
            get = pltpu.make_async_copy((up_hbm if side else lo_hbm).at[b // 2], halo.at[side * HALO + h], sem.at[1 + side * HALO + h])
            get.start()
            sides.append((get, there, b % 2))

    def clear(i, _):
        acc[i] = jnp.zeros((24, LANES), jnp.float32)
        return 0
    lax.fori_loop(0, blocks, clear, 0, unroll=8)
    tab_j[2 * HALO + blocks] = jnp.zeros(tab_j.shape[1:], jnp.float32)
    tab_r[2 * HALO + blocks] = jnp.zeros(tab_r.shape[1:], jnp.float32)

    picks, halves = pickers()
    kind = lax.broadcasted_iota(jnp.int32, (8, LANES), 0)
    factor = jnp.where(kind < 3, 1.0, jnp.where(kind < 6, ROOT, jnp.where(kind == 6, -1.0, 1.0)))

    get_own.wait()

    def own(t, _):
        m8 = pm_ref[t] * factor
        out = spread(m8[3:6], (0, 1), picks, halves)
        for h in range(2):
            for c in range(3):
                s = 96 * h + 32 * c
                tab_j[HALO + 2 * t + h, c] = out[s:s + 32]
        turned = pltpu.roll(m8, 64, 1)
        for h in range(2):
            both = jnp.where(left1, m8, turned) if h == 0 else jnp.where(left1, turned, m8)
            for c in range(4):
                tab_i[2 * t + h, c] = jnp.broadcast_to(both[3 + c:4 + c], (8, LANES))
        return 0
    lax.fori_loop(0, chunks, own, 0, unroll=16)

    for get, _, _ in sides:
        get.wait()
    for n_, (get, there, half) in enumerate(sides):
        e = n_ if n_ < HALO else blocks + n_
        m8 = jnp.where(there, halo[n_], 0.0) * factor
        m8 = jnp.where(half == 1, pltpu.roll(m8, 64, 1), m8)
        out = spread(m8[3:8], (0,), picks, halves)
        for c in range(5):
            (tab_j if c < 3 else tab_r)[e, c % 3] = out[32 * c:32 * c + 32]
    get_range.wait()

    live = count_ref[0]

    def pair(p):
        i = pairs_ref[0, p]
        j = jnp.where(p < live, pairs_ref[1, p], 2 * HALO + blocks)
        xi, yi, zi, ri = (tab_i[i, c] for c in range(4))
        f = [None] * 3
        for g in range(4):
            s = pl.ds(8 * g, 8)
            dx = xi - tab_j[j, 0, s]
            dy = yi - tab_j[j, 1, s]
            dz = zi - tab_j[j, 2, s]
            d = dx * dx + dy * dy + dz * dz
            inv = 1.0 / (ri + tab_r[j, 0, s])
            w = jnp.exp2(d * inv) * (inv * tab_r[j, 1, s])
            for k, v in enumerate((dx, dy, dz)):
                f[k] = w * v if g == 0 else f[k] + w * v
        return i, f

    def group(g, _):
        for u in range(UNROLL):
            i, f = pair(g * UNROLL + u)
            for k in range(3):
                acc[i, pl.ds(8 * k, 8)] = acc[i, pl.ds(8 * k, 8)] + f[k]
        return 0
    lax.fori_loop(0, (live + UNROLL - 1) // UNROLL, group, 0)

    def finish(t, _):
        rows = pm_ref[t]
        scale = (-0.02 / ROOT) * rows[7:8]
        for k in range(3):
            v = [jnp.sum(acc[2 * t + h, pl.ds(8 * k, 8)], axis=0, keepdims=True) for h in range(2)]
            v = [x + pltpu.roll(x, 64, 1) for x in v]
            f = jnp.where(left[0:1], v[0], v[1]) * scale
            at = pl.ds(k * chunks + t, 1)
            pos_ref[at, :] = rows[3 + k:4 + k]
            frc_ref[at, :] = f
            mom_ref[at, :] = rows[k:k + 1] + 0.25 * f
        return 0
    lax.fori_loop(0, chunks, finish, 0, unroll=8)


def force_call(pairs, count, hlo, hup, pm, lo, up, tab):
    chunks = pm.shape[0]
    smem = pl.BlockSpec(memory_space=pltpu.SMEM)
    vmem = pl.BlockSpec(memory_space=pltpu.VMEM)
    hbm = pl.BlockSpec(memory_space=pl.ANY)
    o = jax.ShapeDtypeStruct((3 * chunks, LANES), jnp.float32)
    return pl.pallas_call(
        force_kernel,
        out_shape=(o, o, o),
        in_specs=[smem] * 4 + [hbm] * 4,
        out_specs=(vmem,) * 3,
        scratch_shapes=[
            pltpu.VMEM((2 * chunks + 2 * HALO + 1, 3, 32, LANES), jnp.float32),
            pltpu.VMEM((2 * chunks + 2 * HALO + 1, 2, 32, LANES), jnp.float32),
            pltpu.VMEM((2 * chunks, 4, 8, LANES), jnp.float32),
            pltpu.VMEM((2 * chunks, 24, LANES), jnp.float32),
            pltpu.VMEM((chunks, 8, LANES), jnp.float32),
            pltpu.VMEM((2 * HALO, 8, LANES), jnp.float32),
            pltpu.SemaphoreType.DMA((2 + 2 * HALO,)),
        ],
        compiler_params=pltpu.CompilerParams(vmem_limit_bytes=60 * 2**20),
        name="pair_forces",
    )(pairs, count, hlo, hup, pm, lo, up, tab)


def shards(positions, momenta, forces, noise, species, block_pairs, pair_count, halo_blocks):
    flat = [a.reshape(-1, LANES) for a in (positions, momenta, forces, noise)]
    pm, lo, up, hlo, hup, tab = exchange(*flat, species.reshape(-1, LANES), halo_blocks)
    outs = force_call(block_pairs, pair_count, hlo, hup, pm, lo, up, tab)
    return tuple(o.reshape(positions.shape) for o in outs)


def solution(mesh):
    big = P("bead", None, "space")
    in_specs = (big, big, big, big, P("space"), P(None, "space"), P("space"), P(None, "space"))
    return jax.shard_map(shards, mesh=mesh, in_specs=in_specs, out_specs=(big, big, big), check_vma=False)
```
